32 devices in a mesh: worker: 2 (over x), shard: 16 (over z, y, core).
Axes of the slice: x: 2, y: 2, z: 4, core: 2. Of those that a mesh axis runs over, the one named last changes fastest.
Arguments:
- acts: bfloat16 [16384, 8192], P(('worker', 'shard')), may hold values from -6 to 6
- out_grads: bfloat16 [16384, 1024], P(('worker', 'shard')), may hold values from -6 to 6
- local_weight: bfloat16 [2, 1024, 8192], P('worker', 'shard'), may hold values from -6.1 to 6.1
- adam_mean: float32 [2, 1024, 8192], P('worker', 'shard'), may hold values from -0.6 to 0.6
- adam_var: float32 [2, 1024, 8192], P('worker', 'shard'), may hold values from 0.05 to 2
- global_weight: float32 [1024, 8192], P('shard', 'worker'), may hold values from -6 to 6
- outer_momentum: float32 [1024, 8192], P('shard', 'worker'), may hold values from -0.12 to 0.12
- step_count: int32 [1], replicated, may hold values from 1 to 8
Outputs:
- synced_weight: bfloat16 [1024, 8192], P('shard')
- new_global: float32 [1024, 8192], P('shard', 'worker')
- new_momentum: float32 [1024, 8192], P('shard', 'worker')
The draws below stay inside these ranges and needn't reach their ends.
All inputs are finite; a program needn't handle non-finite values.
Results may differ from the reference program's by a relative error of at most 0.012.
Values may be sent and summed in bfloat16 or wider, within the bound.
A program may use at most 128 MiB of HBM per device.

```python
import math
import jax
import jax.numpy as jnp
from jax import lax

D = 8192
KV = 1024
TOK_DEV = 512
TOKENS = 16384
N_WORKER = 2
N_SHARD = 16


def shared_anchor(key):
    return jnp.clip(jax.random.normal(key, (KV, D), jnp.float32), -6.0, 6.0)


def draw_global_weight(key, part):
    anchor = shared_anchor(key)
    return anchor.astype(jnp.float32)


def draw_local_weight(key, part):
    anchor = shared_anchor(key)
    key = jax.random.fold_in(key, 5)
    drift = jnp.clip(0.015 * jax.random.normal(key, (N_WORKER, KV, D), jnp.float32), -0.09, 0.09)
    return (anchor[None] + drift).astype(jnp.bfloat16)


def with_spikes(array, own_key, source, target, blocks, factor):
    def block_of(dim):
        return (jnp.arange(array.shape[dim]) // (array.shape[dim] // blocks)).reshape((-1,) + (1,) * (array.ndim - 1 - dim))

    near = jax.random.permutation(own_key, blocks)[block_of(target)]
    other_side = (block_of(target) + blocks // 2) % blocks
    return jnp.where((block_of(source) == near) | (block_of(source) == other_side), factor * array, array)


def block_scale(key, shape, pieces, least, largest):
    level = 1.0
    for position, blocks in pieces:
        draws = jax.random.uniform(jax.random.fold_in(jax.random.fold_in(key, 6), position), (blocks,), jnp.float32, least / len(pieces), largest / len(pieces))
        level = level * jnp.repeat(jnp.exp(draws), shape[position] // blocks).reshape((-1,) + (1,) * (len(shape) - 1 - position))
    return level


def bell_draw(rng, shape, deviation, limit, pieces=(), dtype=jnp.bfloat16):
    result = deviation * jax.random.normal(rng, shape, jnp.float32)
    if pieces:
        result = result * block_scale(rng, shape, pieces, -0.22, 0.18)
    return jnp.clip(result, -limit, limit).astype(dtype)


def gaussian_with(rng, extent, deviation, bound, shards, heavy, dtype=jnp.bfloat16):
    result = deviation * jax.random.normal(rng, extent, jnp.float32)
    if shards:
        result = result * block_scale(rng, extent, shards, -0.22, 0.18)
    return jnp.clip(with_spikes(result, jax.random.fold_in(rng, 3), *heavy), -bound, bound).astype(dtype)


def setup_inputs(seed: int = 0) -> dict:
    arg_keys = jax.random.split(jax.random.key(seed), 9)
    acts = bell_draw(arg_keys[0], (TOKENS, D), 1.0, 6.0, ((0, 32),))
    out_grads = gaussian_with(arg_keys[1], (TOKENS, KV), 1.0, 6.0, ((0, 32),), (0, 1, 32, 2.75))
    local_weight = draw_local_weight(jax.random.fold_in(arg_keys[8], 71), 0)
    adam_mean = bell_draw(arg_keys[3], (N_WORKER, KV, D), 0.1, 0.6, ((0, 2), (1, 16)), jnp.float32)
    adam_var = jnp.clip(jnp.exp(math.log(2.0) - 3.6888794 * jax.random.uniform(arg_keys[4], (N_WORKER, KV, D), jnp.float32) ** block_scale(arg_keys[4], (N_WORKER, KV, D), ((0, 2), (1, 16)), -0.2, 0.2)), 0.05, 2.0)
    global_weight = draw_global_weight(jax.random.fold_in(arg_keys[8], 71), 0)
    outer_momentum = bell_draw(arg_keys[6], (KV, D), 0.02, 0.12, ((0, 16), (1, 2)), jnp.float32)
    step_count = jax.random.randint(arg_keys[7], (1,), 1, 9).astype(jnp.int32)
    return {"acts": acts, "out_grads": out_grads, "local_weight": local_weight, "adam_mean": adam_mean, "adam_var": adam_var, "global_weight": global_weight, "outer_momentum": outer_momentum, "step_count": step_count}


def inner_step(weight, mean, var, grad, count):
    moment = 0.9 * mean + 0.1 * grad
    second = 0.95 * var + 0.05 * grad * grad
    first_fix = 1.0 - jnp.power(0.9, count)
    second_fix = 1.0 - jnp.power(0.95, count)
    ratio = moment / first_fix / (jnp.sqrt(second / second_fix) + 1e-08)
    return weight - 0.1 * (ratio + 0.1 * weight)

def reference(acts, out_grads, local_weight, adam_mean, adam_var, global_weight, outer_momentum, step_count):
    wtok = TOK_DEV * N_SHARD
    factor = 1.0 / math.sqrt(wtok)
    count = step_count[0].astype(jnp.float32)
    total = jnp.zeros((KV, D), jnp.float32)
    for replica in range(N_WORKER):
        inputs = acts[replica * wtok:(replica + 1) * wtok].reshape(N_SHARD, TOK_DEV, D)
        upstream = out_grads[replica * wtok:(replica + 1) * wtok].reshape(N_SHARD, TOK_DEV, KV)

        def add_block(carry, pair):
            block_in, block_up = pair
            term = lax.dot_general(block_up, block_in, (((0,), (0,)), ((), ())), preferred_element_type=jnp.float32) * factor
            term = lax.optimization_barrier(term.astype(jnp.bfloat16))
            return (carry + term.astype(jnp.float32), None)
        grad, _ = lax.scan(add_block, jnp.zeros((KV, D), jnp.float32), (inputs, upstream))
        weight = local_weight[replica].astype(jnp.float32)
        total = total + inner_step(weight, adam_mean[replica], adam_var[replica], grad, count)
    delta = global_weight - total / N_WORKER
    new_momentum = 0.9 * outer_momentum + delta
    new_global = global_weight - 0.7 * (delta + 0.9 * new_momentum)
    return (new_global.astype(jnp.bfloat16), new_global, new_momentum)
```

```python
import functools
import math

import jax
import jax.numpy as jnp
from jax import lax
from jax.experimental import pallas as pl
from jax.experimental.pallas import tpu as pltpu
from jax.sharding import PartitionSpec as P

CORES = 2
ROWS_Y = 2
LAYERS_Z = 4
CHUNKS = 16
LAG_Y = 3
LAG_Z = 5
LAG_CORE = 6
LAG_RATIO = 7


def inner_step(weight, mean, var, grad, count):
    moment = 0.9 * mean + 0.1 * grad
    second = 0.95 * var + 0.05 * grad * grad
    first_fix = 1.0 - jnp.power(0.9, count)
    second_fix = 1.0 - jnp.power(0.95, count)
    ratio = moment / first_fix / (jnp.sqrt(second / second_fix) + 1e-08)
    return weight - 0.1 * (ratio + 0.1 * weight)


def plain(
    acts, out_grads, local_weight, adam_mean, adam_var, global_weight, outer_momentum, step_count
):
    shards = lax.axis_size("shard")
    workers = lax.axis_size("worker")
    factor = 1.0 / math.sqrt(acts.shape[0] * shards)
    count = step_count[0].astype(jnp.float32)
    term = lax.dot_general(
        out_grads, acts, (((0,), (0,)), ((), ())), preferred_element_type=jnp.float32
    )
    grad = lax.psum_scatter(
        (term * factor).astype(jnp.bfloat16), "shard", scatter_dimension=0, tiled=True
    ).astype(jnp.float32)
    weight = local_weight[0].astype(jnp.float32)
    stepped = inner_step(weight, adam_mean[0], adam_var[0], grad, count)
    summed = lax.psum_scatter(stepped, "worker", scatter_dimension=1, tiled=True)
    delta = global_weight - summed / workers
    momentum = 0.9 * outer_momentum + delta
    updated = global_weight - 0.7 * (delta + 0.9 * momentum)
    synced = lax.all_gather(updated.astype(jnp.bfloat16), "worker", axis=1, tiled=True)
    return (synced, updated, momentum)


def kernel(
    factor, acts, grads, weight, mean, var, glob, outer, count,
    synced, new_glob, new_mom,
    a, g, gt, p, yin, zin, cout, gbuf, rout, rin, acc, ng, nm, sy, wv, mv, vv, gv, ov, wo,
    a_loc, a_out, a_in, gt_out, gt_in, y_out, y_in, z_out, z_in, c_out, c_in, r_out, r_in,
    s_out, s_in, w_out, w_in, loads, stores,
):
    r = lax.axis_index("worker")
    s = lax.axis_index("shard")
    z = lax.div(s, 4)
    y = lax.rem(lax.div(s, 2), 2)
    k = lax.rem(s, 2)
    tokens = acts.shape[0]
    chunks, _, cols = a.shape
    half = chunks * cols
    rows = yin.shape[1]
    units = gbuf.shape[2]
    block = CORES * units
    other_core = (r, z * 4 + y * 2 + 1 - k)
    other_y = (r, z * 4 + (1 - y) * 2 + k)
    other_worker = (1 - r, s)
    zs = [lax.rem(z + d, 4) for d in (1, 2, 3)]
    others_z = [(r, t * 4 + y * 2 + k) for t in zs]

    def remote(src, dst, send, recv, to):
        return pltpu.make_async_remote_copy(
            src_ref=src, dst_ref=dst, send_sem=send, recv_sem=recv,
            device_id=to, device_id_type=pl.DeviceIdType.MESH,
        )

    def at(start, step=cols):
        return pl.ds(pl.multiple_of(start, step), step)

    def acts_local(c):
        return pltpu.make_async_copy(
            acts.at[:, at(k * half + c * cols)], a.at[c, pl.ds(0, tokens)], a_loc.at[c]
        )

    def acts_remote(c):
        return remote(
            acts.at[:, at((1 - k) * half + c * cols)], a.at[c, pl.ds(tokens, tokens)],
            a_out.at[c], a_in.at[c], other_core,
        )

    def y_copy(c):
        return remote(
            p.at[c, at((1 - y) * rows, rows)], yin.at[c], y_out.at[c], y_in.at[c], other_y
        )

    def z_copy(c, d):
        return remote(
            p.at[c, at(y * rows + zs[d] * block, block)], zin.at[c, d],
            z_out.at[c, d], z_in.at[c, d], others_z[d],
        )

    def core_copy(c):
        return remote(cout.at[c], gbuf.at[c, k], c_out.at[c], c_in.at[c], other_core)

    def ratio_copy(c):
        return remote(rout.at[c], rin.at[c], r_out.at[c], r_in.at[c], other_worker)

    def synced_copy(c):
        return remote(
            sy.at[c], synced.at[:, at(r * half + c * cols)], s_out.at[c], s_in.at[c], other_worker
        )

    def stores_of(c):
        return [
            pltpu.make_async_copy(sy.at[c], synced.at[:, at(r * half + c * cols)], stores.at[0, c]),
            pltpu.make_async_copy(ng.at[c], new_glob.at[:, at(c * cols)], stores.at[1, c]),
            pltpu.make_async_copy(nm.at[c], new_mom.at[:, at(c * cols)], stores.at[2, c]),
        ]

    grads_in = pltpu.make_async_copy(grads, g, loads.at[0])
    grads_in.start()

    @pl.loop(0, chunks)
    def _(c):
        acts_local(c).start()

    others = [
        pltpu.make_async_copy(x, v, loads.at[1 + j])
        for j, (x, v) in enumerate(
            ((weight, wv), (mean, mv), (var, vv), (glob, gv), (outer, ov))
        )
    ]
    for copy in others:
        copy.start()

    barrier = pltpu.get_barrier_semaphore()
    for peer in (other_core, other_y, other_worker, *others_z):
        pl.semaphore_signal(barrier, inc=1, device_id=peer, device_id_type=pl.DeviceIdType.MESH)
    pl.semaphore_wait(barrier, 6)

    @pl.loop(0, chunks)
    def _(c):
        acts_remote(c).start()

    weight_copy = remote(
        weight.at[:, at((1 - r) * half, half)], wo, w_out, w_in, other_worker
    )
    weight_copy.start()

    grads_in.wait()
    for j in range(g.shape[1] // block):
        place = (j % ROWS_Y) * LAYERS_Z + j // ROWS_Y
        gt[place * block : (place + 1) * block, 0:tokens] = g[:, j * block : (j + 1) * block].T
    gt_copy = remote(
        gt.at[:, pl.ds(0, tokens)], gt.at[:, pl.ds(tokens, tokens)], gt_out, gt_in, other_core
    )
    gt_copy.start()
    for copy in others:
        copy.wait()
    gt_copy.wait_recv()
    weight_copy.wait_recv()

    time = jnp.full((1, cols), count[0].astype(jnp.float32))
    first = 1.0 / (1.0 - jnp.exp(time * math.log(0.9)))
    second_inv = 1.0 / (1.0 - jnp.exp(time * math.log(0.95)))

    def ratio_of(c, side):
        where = at(side * half + c * cols)
        grad = gbuf[c, side].astype(jnp.float32) * factor
        moment = 0.9 * mv[:, where] + 0.1 * grad
        second = 0.95 * vv[:, where] + 0.05 * grad * grad
        return moment * first / (jnp.sqrt(second * second_inv) + 1e-08)

    def product(c, side):
        p[c, at(side * rows, rows)] = jnp.dot(
            gt[at(side * rows, rows)], a[c], preferred_element_type=jnp.float32
        ).astype(jnp.bfloat16)

    @pl.loop(0, chunks + LAG_RATIO)
    def _(i):
        @pl.when(i < chunks)
        def _():
            c = i
            acts_local(c).wait()
            acts_remote(c).wait_recv()
            product(c, 1 - y)
            y_copy(c).start()
            product(c, y)

        @pl.when((i >= LAG_Y) & (i < chunks + LAG_Y))
        def _():
            c = i - LAG_Y
            y_copy(c).wait_recv()
            mine = at(y * rows, rows)
            p[c, mine] = (
                p[c, mine].astype(jnp.float32) + yin[c].astype(jnp.float32)
            ).astype(jnp.bfloat16)
            for d in (1, 0, 2):
                z_copy(c, d).start()

        @pl.when((i >= LAG_Z) & (i < chunks + LAG_Z))
        def _():
            c = i - LAG_Z
            for d in range(3):
                z_copy(c, d).wait_recv()

            def total(core):
                part = at(core * units, units)
                value = p[c, at(y * rows + z * block + core * units, units)].astype(jnp.float32)
                for d in range(3):
                    value += zin[c, d, part].astype(jnp.float32)
                return value.astype(jnp.bfloat16)

            cout[c] = total(1 - k)
            core_copy(c).start()
            gbuf[c, k] = total(k)

        @pl.when((i >= LAG_CORE) & (i < chunks + LAG_CORE))
        def _():
            c = i - LAG_CORE
            core_copy(c).wait_recv()
            rout[c] = ratio_of(c, 1 - r).astype(jnp.bfloat16)
            ratio_copy(c).start()
            own = wv[:, at(r * half + c * cols)].astype(jnp.float32)
            acc[c] = own - 0.1 * (ratio_of(c, r) + 0.1 * own)

        @pl.when(i >= LAG_RATIO)
        def _():
            c = i - LAG_RATIO
            ratio_copy(c).wait_recv()
            where = at(c * cols)
            its = wo[:, where].astype(jnp.float32)
            summed = acc[c] + (its - 0.1 * (rin[c].astype(jnp.float32) + 0.1 * its))
            delta = gv[:, where] - summed * 0.5
            momentum = 0.9 * ov[:, where] + delta
            updated = gv[:, where] - 0.7 * (delta + 0.9 * momentum)
            sy[c] = updated.astype(jnp.bfloat16)
            synced_copy(c).start()
            ng[c] = updated
            nm[c] = momentum
            for copy in stores_of(c):
                copy.start()

    weight_copy.wait_send()
    gt_copy.wait_send()

    @pl.loop(0, chunks)
    def _(c):
        acts_remote(c).wait_send()
        y_copy(c).wait_send()
        for d in range(3):
            z_copy(c, d).wait_send()
        core_copy(c).wait_send()
        ratio_copy(c).wait_send()
        synced_copy(c).wait()
        for copy in stores_of(c):
            copy.wait()


def fused(
    acts, out_grads, local_weight, adam_mean, adam_var, global_weight, outer_momentum, step_count
):
    tokens, width = acts.shape
    features = out_grads.shape[1]
    units = local_weight.shape[1]
    half = width // CORES
    cols = half // CHUNKS
    rows = features // ROWS_Y
    factor = 1.0 / math.sqrt(tokens * lax.axis_size("shard"))
    b16, f32 = jnp.bfloat16, jnp.float32
    vmem, dma = pltpu.VMEM, pltpu.SemaphoreType.DMA
    n = CHUNKS
    return pl.pallas_call(
        functools.partial(kernel, factor),
        out_shape=(
            jax.ShapeDtypeStruct((units, width), b16),
            jax.ShapeDtypeStruct((units, half), f32),
            jax.ShapeDtypeStruct((units, half), f32),
        ),
        in_specs=[pl.BlockSpec(memory_space=pl.ANY)] * 7
        + [pl.BlockSpec(memory_space=pltpu.SMEM)],
        out_specs=[pl.BlockSpec(memory_space=pl.ANY)] * 3,
        scratch_shapes=[
            vmem((n, CORES * tokens, cols), b16),
            vmem((tokens, features), b16),
            vmem((features, CORES * tokens), b16),
            vmem((n, features, cols), b16),
            vmem((n, rows, cols), b16),
            vmem((n, LAYERS_Z - 1, CORES * units, cols), b16),
            vmem((n, units, cols), b16),
            vmem((n, CORES, units, cols), b16),
            vmem((n, units, cols), b16),
            vmem((n, units, cols), b16),
            vmem((n, units, cols), f32),
            vmem((n, units, cols), f32),
            vmem((n, units, cols), f32),
            vmem((n, units, cols), b16),
            vmem((units, width), b16),
            vmem((units, width), f32),
            vmem((units, width), f32),
            vmem((units, half), f32),
            vmem((units, half), f32),
            vmem((units, half), b16),
            dma((n,)), dma((n,)), dma((n,)), dma, dma,
            dma((n,)), dma((n,)), dma((n, 3)), dma((n, 3)),
            dma((n,)), dma((n,)), dma((n,)), dma((n,)),
            dma((n,)), dma((n,)), dma, dma, dma((6,)), dma((3, n)),
        ],
        compiler_params=pltpu.CompilerParams(
            collective_id=0, has_side_effects=True, vmem_limit_bytes=56 * 2**20
        ),
        cost_estimate=pl.CostEstimate(
            flops=2 * tokens * width * features, bytes_accessed=24 * 2**20, transcendentals=0
        ),
    )(
        acts, out_grads, local_weight[0], adam_mean[0], adam_var[0],
        global_weight, outer_momentum, step_count,
    )


def solution(mesh):
    placed = (
        P(("worker", "shard"), None),
        P(("worker", "shard"), None),
        P("worker", "shard", None),
        P("worker", "shard", None),
        P("worker", "shard", None),
        P("shard", "worker"),
        P("shard", "worker"),
        P(),
    )
    grid = (2, CORES * ROWS_Y * LAYERS_Z)
    return jax.shard_map(
        fused if (mesh.shape["worker"], mesh.shape["shard"]) == grid else plain,
        mesh=mesh,
        in_specs=placed,
        out_specs=(P("shard", None), P("shard", "worker"), P("shard", "worker")),
        check_vma=False,
    )
```

```python
import functools
import math

import jax
import jax.numpy as jnp
from jax import lax
from jax.experimental import pallas as pl
from jax.experimental.pallas import tpu as pltpu
from jax.sharding import PartitionSpec as P

CORES = 2
ROWS_Y = 2
LAYERS_Z = 4
CHUNKS = 16
LAG_Y = 3
LAG_Z = 5
LAG_CORE = 6
LAG_RATIO = 7
LAG_DONE = 8


def inner_step(weight, mean, var, grad, count):
    moment = 0.9 * mean + 0.1 * grad
    second = 0.95 * var + 0.05 * grad * grad
    first_fix = 1.0 - jnp.power(0.9, count)
    second_fix = 1.0 - jnp.power(0.95, count)
    ratio = moment / first_fix / (jnp.sqrt(second / second_fix) + 1e-08)
    return weight - 0.1 * (ratio + 0.1 * weight)


def plain(
    acts, out_grads, local_weight, adam_mean, adam_var, global_weight, outer_momentum, step_count
):
    shards = lax.axis_size("shard")
    workers = lax.axis_size("worker")
    factor = 1.0 / math.sqrt(acts.shape[0] * shards)
    count = step_count[0].astype(jnp.float32)
    term = lax.dot_general(
        out_grads, acts, (((0,), (0,)), ((), ())), preferred_element_type=jnp.float32
    )
    grad = lax.psum_scatter(
        (term * factor).astype(jnp.bfloat16), "shard", scatter_dimension=0, tiled=True
    ).astype(jnp.float32)
    weight = local_weight[0].astype(jnp.float32)
    stepped = inner_step(weight, adam_mean[0], adam_var[0], grad, count)
    summed = lax.psum_scatter(stepped, "worker", scatter_dimension=1, tiled=True)
    delta = global_weight - summed / workers
    momentum = 0.9 * outer_momentum + delta
    updated = global_weight - 0.7 * (delta + 0.9 * momentum)
    synced = lax.all_gather(updated.astype(jnp.bfloat16), "worker", axis=1, tiled=True)
    return (synced, updated, momentum)


def kernel(
    factor, acts, grads, weight, mean, var, glob, outer, count,
    synced, new_glob, new_mom,
    a, g, gt, p, yin, zin, cout, gbuf, rout, rin, acc, ng, nm, sy, wv, mv, vv, gv, ov, wo,
    a_loc, a_out, a_in, gt_out, gt_in, y_out, y_in, z_out, z_in, c_out, c_in, r_out, r_in,
    s_out, s_in, w_out, w_in, loads, stores,
):
    r = lax.axis_index("worker")
    s = lax.axis_index("shard")
    z = lax.div(s, 4)
    y = lax.rem(lax.div(s, 2), 2)
    k = lax.rem(s, 2)
    tokens = acts.shape[0]
    chunks, _, cols = a.shape
    half = chunks * cols
    rows = yin.shape[1]
    units = gbuf.shape[2]
    block = CORES * units
    other_core = (r, z * 4 + y * 2 + 1 - k)
    other_y = (r, z * 4 + (1 - y) * 2 + k)
    other_worker = (1 - r, s)
    zs = [lax.rem(z + d, 4) for d in (1, 2, 3)]
    others_z = [(r, t * 4 + y * 2 + k) for t in zs]

    def remote(src, dst, send, recv, to):
        return pltpu.make_async_remote_copy(
            src_ref=src, dst_ref=dst, send_sem=send, recv_sem=recv,
            device_id=to, device_id_type=pl.DeviceIdType.MESH,
        )

    def at(start, step=cols):
        return pl.ds(pl.multiple_of(start, step), step)

    def acts_local(c):
        return pltpu.make_async_copy(
            acts.at[:, at(k * half + c * cols)], a.at[c, pl.ds(0, tokens)], a_loc.at[c]
        )

    def acts_remote(c):
        return remote(
            acts.at[:, at((1 - k) * half + c * cols)], a.at[c, pl.ds(tokens, tokens)],
            a_out.at[c], a_in.at[c], other_core,
        )

    def y_copy(c):
        return remote(
            p.at[c, at((1 - y) * rows, rows)], yin.at[c], y_out.at[c], y_in.at[c], other_y
        )

    def z_copy(c, d):
        return remote(
            p.at[c, at(y * rows + zs[d] * block, block)], zin.at[c, d],
            z_out.at[c, d], z_in.at[c, d], others_z[d],
        )

    def core_copy(c):
        return remote(cout.at[c], gbuf.at[c, k], c_out.at[c], c_in.at[c], other_core)

    def ratio_copy(c):
        return remote(rout.at[c], rin.at[c], r_out.at[c], r_in.at[c], other_worker)

    def synced_copy(c):
        return remote(
            sy.at[c], synced.at[:, at(r * half + c * cols)], s_out.at[c], s_in.at[c], other_worker
        )

    def stores_of(c):
        return [
            pltpu.make_async_copy(sy.at[c], synced.at[:, at(r * half + c * cols)], stores.at[0, c]),
            pltpu.make_async_copy(ng.at[c], new_glob.at[:, at(c * cols)], stores.at[1, c]),
            pltpu.make_async_copy(nm.at[c], new_mom.at[:, at(c * cols)], stores.at[2, c]),
        ]

    grads_in = pltpu.make_async_copy(grads, g, loads.at[0])
    grads_in.start()

    @pl.loop(0, chunks)
    def _(c):
        acts_local(c).start()

    others = [
        pltpu.make_async_copy(x, v, loads.at[1 + j])
        for j, (x, v) in enumerate(
            ((weight, wv), (mean, mv), (var, vv), (glob, gv), (outer, ov))
        )
    ]
    for copy in others:
        copy.start()

    barrier = pltpu.get_barrier_semaphore()
    for peer in (other_core, other_y, other_worker, *others_z):
        pl.semaphore_signal(barrier, inc=1, device_id=peer, device_id_type=pl.DeviceIdType.MESH)

    grads_in.wait()
    for j in range(g.shape[1] // block):
        place = (j % ROWS_Y) * LAYERS_Z + j // ROWS_Y
        gt[place * block : (place + 1) * block, 0:tokens] = g[:, j * block : (j + 1) * block].T
    gt_copy = remote(
        gt.at[:, pl.ds(0, tokens)], gt.at[:, pl.ds(tokens, tokens)], gt_out, gt_in, other_core
    )
    weight_copy = remote(
        weight.at[:, at((1 - r) * half, half)], wo, w_out, w_in, other_worker
    )
    pl.semaphore_wait(barrier, 6)
    gt_copy.start()

    @pl.loop(0, chunks)
    def _(c):
        acts_remote(c).start()

    weight_copy.start()
    gt_copy.wait_recv()

    time = jnp.full((1, cols), count[0].astype(jnp.float32))
    first = 1.0 / (1.0 - jnp.exp(time * math.log(0.9)))
    second_inv = 1.0 / (1.0 - jnp.exp(time * math.log(0.95)))

    def ratio_of(c, side):
        where = at(side * half + c * cols)
        grad = gbuf[c, side].astype(jnp.float32) * factor
        moment = 0.9 * mv[:, where] + 0.1 * grad
        second = 0.95 * vv[:, where] + 0.05 * grad * grad
        return moment * first / (jnp.sqrt(second * second_inv) + 1e-08)

    def product(c, side):
        p[c, at(side * rows, rows)] = jnp.dot(
            gt[at(side * rows, rows)], a[c], preferred_element_type=jnp.float32
        ).astype(jnp.bfloat16)

    @pl.loop(0, chunks + LAG_DONE)
    def _(i):
        @pl.when(i < chunks)
        def _():
            c = i
            acts_local(c).wait()
            acts_remote(c).wait_recv()
            product(c, 1 - y)
            y_copy(c).start()
            product(c, y)

        @pl.when((i >= LAG_Y) & (i < chunks + LAG_Y))
        def _():
            c = i - LAG_Y
            y_copy(c).wait_recv()
            mine = at(y * rows, rows)
            p[c, mine] = (
                p[c, mine].astype(jnp.float32) + yin[c].astype(jnp.float32)
            ).astype(jnp.bfloat16)
            for d in (1, 0, 2):
                z_copy(c, d).start()

        @pl.when((i >= LAG_Z) & (i < chunks + LAG_Z))
        def _():
            c = i - LAG_Z
            for d in range(3):
                z_copy(c, d).wait_recv()

            def total(core):
                part = at(core * units, units)
                value = p[c, at(y * rows + z * block + core * units, units)].astype(jnp.float32)
                for d in range(3):
                    value += zin[c, d, part].astype(jnp.float32)
                return value.astype(jnp.bfloat16)

            cout[c] = total(1 - k)
            core_copy(c).start()
            gbuf[c, k] = total(k)

        @pl.when(i == LAG_CORE)
        def _():
            for copy in others:
                copy.wait()
            weight_copy.wait()

        @pl.when((i >= LAG_CORE) & (i < chunks + LAG_CORE))
        def _():
            c = i - LAG_CORE
            core_copy(c).wait_recv()
            rout[c] = ratio_of(c, 1 - r).astype(jnp.bfloat16)
            ratio_copy(c).start()
            own = wv[:, at(r * half + c * cols)].astype(jnp.float32)
            acc[c] = own - 0.1 * (ratio_of(c, r) + 0.1 * own)

        @pl.when((i >= LAG_RATIO) & (i < chunks + LAG_RATIO))
        def _():
            c = i - LAG_RATIO
            ratio_copy(c).wait_recv()
            where = at(c * cols)
            its = wo[:, where].astype(jnp.float32)
            summed = acc[c] + (its - 0.1 * (rin[c].astype(jnp.float32) + 0.1 * its))
            delta = gv[:, where] - summed * 0.5
            momentum = 0.9 * ov[:, where] + delta
            updated = gv[:, where] - 0.7 * (delta + 0.9 * momentum)
            sy[c] = updated.astype(jnp.bfloat16)
            synced_copy(c).start()
            ng[c] = updated
            nm[c] = momentum
            for copy in stores_of(c):
                copy.start()

        @pl.when(i >= LAG_DONE)
        def _():
            c = i - LAG_DONE
            acts_remote(c).wait_send()
            y_copy(c).wait_send()
            for d in range(3):
                z_copy(c, d).wait_send()
            core_copy(c).wait_send()
            ratio_copy(c).wait_send()
            synced_copy(c).wait()
            for copy in stores_of(c):
                copy.wait()

    gt_copy.wait_send()


def fused(
    acts, out_grads, local_weight, adam_mean, adam_var, global_weight, outer_momentum, step_count
):
    tokens, width = acts.shape
    features = out_grads.shape[1]
    units = local_weight.shape[1]
    half = width // CORES
    cols = half // CHUNKS
    rows = features // ROWS_Y
    factor = 1.0 / math.sqrt(tokens * lax.axis_size("shard"))
    b16, f32 = jnp.bfloat16, jnp.float32
    vmem, dma = pltpu.VMEM, pltpu.SemaphoreType.DMA
    n = CHUNKS
    return pl.pallas_call(
        functools.partial(kernel, factor),
        out_shape=(
            jax.ShapeDtypeStruct((units, width), b16),
            jax.ShapeDtypeStruct((units, half), f32),
            jax.ShapeDtypeStruct((units, half), f32),
        ),
        in_specs=[pl.BlockSpec(memory_space=pl.ANY)] * 7
        + [pl.BlockSpec(memory_space=pltpu.SMEM)],
        out_specs=[pl.BlockSpec(memory_space=pl.ANY)] * 3,
        scratch_shapes=[
            vmem((n, CORES * tokens, cols), b16),
            vmem((tokens, features), b16),
            vmem((features, CORES * tokens), b16),
            vmem((n, features, cols), b16),
            vmem((n, rows, cols), b16),
            vmem((n, LAYERS_Z - 1, CORES * units, cols), b16),
            vmem((n, units, cols), b16),
            vmem((n, CORES, units, cols), b16),
            vmem((n, units, cols), b16),
            vmem((n, units, cols), b16),
            vmem((n, units, cols), f32),
            vmem((n, units, cols), f32),
            vmem((n, units, cols), f32),
            vmem((n, units, cols), b16),
            vmem((units, width), b16),
            vmem((units, width), f32),
            vmem((units, width), f32),
            vmem((units, half), f32),
            vmem((units, half), f32),
            vmem((units, half), b16),
            dma((n,)), dma((n,)), dma((n,)), dma, dma,
            dma((n,)), dma((n,)), dma((n, 3)), dma((n, 3)),
            dma((n,)), dma((n,)), dma((n,)), dma((n,)),
            dma((n,)), dma((n,)), dma, dma, dma((6,)), dma((3, n)),
        ],
        compiler_params=pltpu.CompilerParams(
            collective_id=0, has_side_effects=True, vmem_limit_bytes=56 * 2**20
        ),
        cost_estimate=pl.CostEstimate(
            flops=2 * tokens * width * features, bytes_accessed=24 * 2**20, transcendentals=0
        ),
    )(
        acts, out_grads, local_weight[0], adam_mean[0], adam_var[0],
        global_weight, outer_momentum, step_count,
    )


def solution(mesh):
    placed = (
        P(("worker", "shard"), None),
        P(("worker", "shard"), None),
        P("worker", "shard", None),
        P("worker", "shard", None),
        P("worker", "shard", None),
        P("shard", "worker"),
        P("shard", "worker"),
        P(),
    )
    grid = (2, CORES * ROWS_Y * LAYERS_Z)
    return jax.shard_map(
        fused if (mesh.shape["worker"], mesh.shape["shard"]) == grid else plain,
        mesh=mesh,
        in_specs=placed,
        out_specs=(P("shard", None), P("shard", "worker"), P("shard", "worker")),
        check_vma=False,
    )
```

```python
import functools
import math

import jax
import jax.numpy as jnp
from jax import lax
from jax.experimental import pallas as pl
from jax.experimental.pallas import tpu as pltpu
from jax.sharding import PartitionSpec as P

CORES = 2
ROWS_Y = 2
LAYERS_Z = 4
CHUNKS = 16
ZFIRST = 2
LAG_Y = 4
LAG_Z = 6
LAG_DONE = 11


def inner_step(weight, mean, var, grad, count):
    moment = 0.9 * mean + 0.1 * grad
    second = 0.95 * var + 0.05 * grad * grad
    first_fix = 1.0 - jnp.power(0.9, count)
    second_fix = 1.0 - jnp.power(0.95, count)
    ratio = moment / first_fix / (jnp.sqrt(second / second_fix) + 1e-08)
    return weight - 0.1 * (ratio + 0.1 * weight)


def plain(
    acts, out_grads, local_weight, adam_mean, adam_var, global_weight, outer_momentum, step_count
):
    shards = lax.axis_size("shard")
    workers = lax.axis_size("worker")
    factor = 1.0 / math.sqrt(acts.shape[0] * shards)
    count = step_count[0].astype(jnp.float32)
    term = lax.dot_general(
        out_grads, acts, (((0,), (0,)), ((), ())), preferred_element_type=jnp.float32
    )
    grad = lax.psum_scatter(
        (term * factor).astype(jnp.bfloat16), "shard", scatter_dimension=0, tiled=True
    ).astype(jnp.float32)
    weight = local_weight[0].astype(jnp.float32)
    stepped = inner_step(weight, adam_mean[0], adam_var[0], grad, count)
    summed = lax.psum_scatter(stepped, "worker", scatter_dimension=1, tiled=True)
    delta = global_weight - summed / workers
    momentum = 0.9 * outer_momentum + delta
    updated = global_weight - 0.7 * (delta + 0.9 * momentum)
    synced = lax.all_gather(updated.astype(jnp.bfloat16), "worker", axis=1, tiled=True)
    return (synced, updated, momentum)


def kernel(
    factor, acts, grads, weight, mean, var, glob, outer, count,
    synced, new_glob, new_mom,
    a, g, gt, p, yin, ybin, lin, rin_z, gbuf, rout, rin, acc, ng, nm, sy, wv, mv, vv, gv, ov, wo,
    a_loc, a_out, a_in, gt_out, gt_in, y_out, y_in, rz_out, rz_in, lz_out, lz_in, c_out, c_in, r_out, r_in,
    s_out, s_in, w_out, w_in, loads, stores,
):
    r = lax.axis_index("worker")
    s = lax.axis_index("shard")
    z = lax.div(s, 4)
    y = lax.rem(lax.div(s, 2), 2)
    k = lax.rem(s, 2)
    tokens = acts.shape[0]
    chunks, _, cols = a.shape
    half = chunks * cols
    rows = yin.shape[1]
    units = gbuf.shape[2]
    block = CORES * units
    other_core = (r, z * 4 + y * 2 + 1 - k)
    other_y = (r, z * 4 + (1 - y) * 2 + k)
    other_worker = (1 - r, s)
    firsts = chunks - yin.shape[0]
    plains = chunks - firsts

    def remote(src, dst, send, recv, to):
        return pltpu.make_async_remote_copy(
            src_ref=src, dst_ref=dst, send_sem=send, recv_sem=recv,
            device_id=to, device_id_type=pl.DeviceIdType.MESH,
        )

    def at(start, step=cols):
        return pl.ds(pl.multiple_of(start, step), step)

    def acts_local(c):
        return pltpu.make_async_copy(
            acts.at[:, at(k * half + c * cols)], a.at[c, pl.ds(0, tokens)], a_loc.at[c]
        )

    def acts_remote(c):
        return remote(
            acts.at[:, at((1 - k) * half + c * cols)], a.at[c, pl.ds(tokens, tokens)],
            a_out.at[c], a_in.at[c], other_core,
        )

    def y_copy(c):
        return remote(
            p.at[c, at((1 - y) * rows, rows)], yin.at[c], y_out.at[c], y_in.at[c], other_y
        )

    def late_y_copy(c):
        return remote(
            p.at[c, at((1 - y) * rows + z * block, block)], ybin.at[c - plains],
            y_out.at[c], y_in.at[c], other_y,
        )

    def right_copy(task, c, part, here):
        size = (LAYERS_Z - 1 - here) * block
        return remote(
            p.at[c, pl.ds(pl.multiple_of(part * rows + (here + 1) * block, block), size)],
            rin_z.at[task, pl.ds(here * block, size)], rz_out.at[task], rz_in.at[task],
            (r, (here + 1) * 4 + y * 2 + k),
        )

    def left_copy(task, c, part, here):
        size = here * block
        return remote(
            p.at[c, pl.ds(pl.multiple_of(part * rows, block), size)],
            lin.at[task, pl.ds(0, size)], lz_out.at[task], lz_in.at[task],
            (r, (here - 1) * 4 + y * 2 + k),
        )

    def add_to(c, part, low, high, *arrived):
        where = pl.ds(pl.multiple_of(part * rows + low * block, block), (high - low) * block)
        value = p[c, where].astype(jnp.float32)
        for ref in arrived:
            value += ref.astype(jnp.float32)
        p[c, where] = value.astype(jnp.bfloat16)

    def from_left(task, low, high):
        return rin_z[task, pl.ds((low - 1) * block, (high - low) * block)]

    def from_right(task, low, high):
        return lin[task, pl.ds(low * block, (high - low) * block)]

    def line_start(task, c, part):
        @pl.when(z == 0)
        def _():
            right_copy(task, c, part, 0).start()

        @pl.when(z == 3)
        def _():
            left_copy(task, c, part, 3).start()

    def line_inward(task, c, part):
        @pl.when(z == 1)
        def _():
            right_copy(task, c, part, 0).wait_recv()
            add_to(c, part, 2, 4, from_left(task, 2, 4))
            right_copy(task, c, part, 1).start()

        @pl.when(z == 2)
        def _():
            left_copy(task, c, part, 3).wait_recv()
            add_to(c, part, 0, 2, from_right(task, 0, 2))
            left_copy(task, c, part, 2).start()

    def line_outward(task, c, part):
        @pl.when(z == 1)
        def _():
            left_copy(task, c, part, 2).wait_recv()
            add_to(c, part, 0, 1, from_right(task, 0, 1))
            left_copy(task, c, part, 1).start()

        @pl.when(z == 2)
        def _():
            right_copy(task, c, part, 1).wait_recv()
            add_to(c, part, 3, 4, from_left(task, 3, 4))
            right_copy(task, c, part, 2).start()

    def line_end(task, c, part):
        @pl.when(z == 0)
        def _():
            left_copy(task, c, part, 1).wait_recv()
            add_to(c, part, 0, 1, from_right(task, 0, 1))

        @pl.when(z == 3)
        def _():
            right_copy(task, c, part, 2).wait_recv()
            add_to(c, part, 3, 4, from_left(task, 3, 4))

        for here in (1, 2):

            @pl.when(z == here)
            def _(here=here):
                add_to(
                    c, part, here, here + 1,
                    from_left(task, here, here + 1), from_right(task, here, here + 1),
                )

    def line_sent(task, c, part):
        for here in range(LAYERS_Z):

            @pl.when(z == here)
            def _(here=here):
                if here < LAYERS_Z - 1:
                    right_copy(task, c, part, here).wait_send()
                if here > 0:
                    left_copy(task, c, part, here).wait_send()

    def core_copy(c):
        return remote(
            p.at[c, at(y * rows + z * block + (1 - k) * units, units)], gbuf.at[c, k],
            c_out.at[c], c_in.at[c], other_core,
        )

    def ratio_copy(c):
        return remote(rout.at[c], rin.at[c], r_out.at[c], r_in.at[c], other_worker)

    def synced_copy(c):
        return remote(
            sy.at[c], synced.at[:, at(r * half + c * cols)], s_out.at[c], s_in.at[c], other_worker
        )

    def stores_of(c):
        return [
            pltpu.make_async_copy(sy.at[c], synced.at[:, at(r * half + c * cols)], stores.at[0, c]),
            pltpu.make_async_copy(ng.at[c], new_glob.at[:, at(c * cols)], stores.at[1, c]),
            pltpu.make_async_copy(nm.at[c], new_mom.at[:, at(c * cols)], stores.at[2, c]),
        ]

    grads_in = pltpu.make_async_copy(grads, g, loads.at[0])
    grads_in.start()

    @pl.loop(0, chunks)
    def _(c):
        acts_local(c).start()

    others = [
        pltpu.make_async_copy(x, v, loads.at[1 + j])
        for j, (x, v) in enumerate(
            ((weight, wv), (mean, mv), (var, vv), (glob, gv), (outer, ov))
        )
    ]
    for copy in others:
        copy.start()

    barrier = pltpu.get_barrier_semaphore()
    for peer in (other_core, other_y, other_worker):
        pl.semaphore_signal(barrier, inc=1, device_id=peer, device_id_type=pl.DeviceIdType.MESH)

    @pl.when(z > 0)
    def _():
        pl.semaphore_signal(
            barrier, inc=1, device_id=(r, s - 4), device_id_type=pl.DeviceIdType.MESH
        )

    @pl.when(z < 3)
    def _():
        pl.semaphore_signal(
            barrier, inc=1, device_id=(r, s + 4), device_id_type=pl.DeviceIdType.MESH
        )

    grads_in.wait()
    for j in range(g.shape[1] // block):
        place = (j % ROWS_Y) * LAYERS_Z + j // ROWS_Y
        gt[place * block : (place + 1) * block, 0:tokens] = g[:, j * block : (j + 1) * block].T
    gt_copy = remote(
        gt.at[:, pl.ds(0, tokens)], gt.at[:, pl.ds(tokens, tokens)], gt_out, gt_in, other_core
    )
    weight_copy = remote(
        weight.at[:, at((1 - r) * half, half)], wo, w_out, w_in, other_worker
    )
    pl.semaphore_wait(barrier, 4 + lax.rem(lax.div(z + 1, 2), 2))
    gt_copy.start()

    acts_remote(0).start()

    @pl.loop(0, firsts)
    def _(j):
        acts_remote(plains + j).start()
        acts_remote(1 + j).start()

    @pl.loop(1 + firsts, plains)
    def _(c):
        acts_remote(c).start()

    weight_copy.start()
    gt_copy.wait_recv()

    time = jnp.full((1, cols), count[0].astype(jnp.float32))
    first = 1.0 / (1.0 - jnp.exp(time * math.log(0.9)))
    second_inv = 1.0 / (1.0 - jnp.exp(time * math.log(0.95)))

    def ratio_of(c, side):
        where = at(side * half + c * cols)
        grad = gbuf[c, side].astype(jnp.float32) * factor
        moment = 0.9 * mv[:, where] + 0.1 * grad
        second = 0.95 * vv[:, where] + 0.05 * grad * grad
        return moment * first / (jnp.sqrt(second * second_inv) + 1e-08)

    def product(c, side):
        p[c, at(side * rows, rows)] = jnp.dot(
            gt[at(side * rows, rows)], a[c], preferred_element_type=jnp.float32
        ).astype(jnp.bfloat16)

    def fetched(c):
        acts_local(c).wait()
        acts_remote(c).wait_recv()

    def to_core(c):
        core_copy(c).start()
        gbuf[c, k] = p[c, at(y * rows + z * block + k * units, units)]

    def adam(c):
        core_copy(c).wait_recv()
        rout[c] = ratio_of(c, 1 - r).astype(jnp.bfloat16)
        ratio_copy(c).start()
        own = wv[:, at(r * half + c * cols)].astype(jnp.float32)
        acc[c] = own - 0.1 * (ratio_of(c, r) + 0.1 * own)

    def update(c):
        ratio_copy(c).wait_recv()
        where = at(c * cols)
        its = wo[:, where].astype(jnp.float32)
        summed = acc[c] + (its - 0.1 * (rin[c].astype(jnp.float32) + 0.1 * its))
        delta = gv[:, where] - summed * 0.5
        momentum = 0.9 * ov[:, where] + delta
        updated = gv[:, where] - 0.7 * (delta + 0.9 * momentum)
        sy[c] = updated.astype(jnp.bfloat16)
        synced_copy(c).start()
        ng[c] = updated
        nm[c] = momentum
        for copy in stores_of(c):
            copy.start()

    def done(c):
        acts_remote(c).wait_send()
        core_copy(c).wait_send()
        ratio_copy(c).wait_send()
        synced_copy(c).wait()
        for copy in stores_of(c):
            copy.wait()

    @pl.loop(0, plains + LAG_DONE)
    def _(i):
        def plain_at(lag):
            def run(stage):
                pl.when((i >= lag) & (i < plains + lag))(lambda: stage(i - lag))
            return run

        def first_at(lag):
            def run(stage):
                pl.when((i >= lag) & (i < firsts + lag))(lambda: stage(i - lag + plains))
            return run

        def halves(stage, c):
            for h in range(ROWS_Y):
                task = plains + (c - plains) * ROWS_Y + h
                stage(task, c, y if h == 1 else 1 - y)

        @plain_at(0)
        def _(c):
            fetched(c)
            product(c, 1 - y)
            y_copy(c).start()
            product(c, y)

        @first_at(1)
        def _(c):
            fetched(c)
            product(c, 1 - y)
            product(c, y)
            halves(line_start, c)

        @plain_at(LAG_Y)
        def _(c):
            y_copy(c).wait_recv()
            add_to(c, y, 0, LAYERS_Z, yin[c])
            line_start(c, c, y)

        @first_at(4)
        def _(c):
            halves(line_inward, c)

        @plain_at(LAG_Z)
        def _(c):
            line_inward(c, c, y)

        @first_at(6)
        def _(c):
            halves(line_outward, c)

        @plain_at(LAG_Z + 1)
        def _(c):
            line_outward(c, c, y)

        @first_at(8)
        def _(c):
            halves(line_end, c)
            late_y_copy(c).start()

        @plain_at(LAG_Z + 2)
        def _(c):
            line_end(c, c, y)
            to_core(c)

        @pl.when(i == LAG_Z + 3)
        def _():
            for copy in others:
                copy.wait()
            weight_copy.wait()

        @plain_at(LAG_Z + 3)
        def _(c):
            adam(c)

        @plain_at(LAG_Z + 4)
        def _(c):
            update(c)

        @plain_at(LAG_DONE)
        def _(c):
            y_copy(c).wait_send()
            line_sent(c, c, y)
            done(c)

        @first_at(12)
        def _(c):
            late_y_copy(c).wait_recv()
            where = at(y * rows + z * block, block)
            p[c, where] = (
                p[c, where].astype(jnp.float32) + ybin[c - plains].astype(jnp.float32)
            ).astype(jnp.bfloat16)
            to_core(c)

        @first_at(13)
        def _(c):
            adam(c)

        @first_at(14)
        def _(c):
            update(c)

        @first_at(15)
        def _(c):
            late_y_copy(c).wait_send()
            halves(line_sent, c)
            done(c)

    gt_copy.wait_send()


def fused(
    acts, out_grads, local_weight, adam_mean, adam_var, global_weight, outer_momentum, step_count
):
    tokens, width = acts.shape
    features = out_grads.shape[1]
    units = local_weight.shape[1]
    half = width // CORES
    cols = half // CHUNKS
    rows = features // ROWS_Y
    factor = 1.0 / math.sqrt(tokens * lax.axis_size("shard"))
    b16, f32 = jnp.bfloat16, jnp.float32
    vmem, dma = pltpu.VMEM, pltpu.SemaphoreType.DMA
    n = CHUNKS
    tasks = n + ZFIRST * (ROWS_Y - 1)
    return pl.pallas_call(
        functools.partial(kernel, factor),
        out_shape=(
            jax.ShapeDtypeStruct((units, width), b16),
            jax.ShapeDtypeStruct((units, half), f32),
            jax.ShapeDtypeStruct((units, half), f32),
        ),
        in_specs=[pl.BlockSpec(memory_space=pl.ANY)] * 7
        + [pl.BlockSpec(memory_space=pltpu.SMEM)],
        out_specs=[pl.BlockSpec(memory_space=pl.ANY)] * 3,
        scratch_shapes=[
            vmem((n, CORES * tokens, cols), b16),
            vmem((tokens, features), b16),
            vmem((features, CORES * tokens), b16),
            vmem((n, features, cols), b16),
            vmem((n - ZFIRST, rows, cols), b16),
            vmem((ZFIRST, CORES * units, cols), b16),
            vmem((tasks, (LAYERS_Z - 1) * CORES * units, cols), b16),
            vmem((tasks, (LAYERS_Z - 1) * CORES * units, cols), b16),
            vmem((n, CORES, units, cols), b16),
            vmem((n, units, cols), b16),
            vmem((n, units, cols), b16),
            vmem((n, units, cols), f32),
            vmem((n, units, cols), f32),
            vmem((n, units, cols), f32),
            vmem((n, units, cols), b16),
            vmem((units, width), b16),
            vmem((units, width), f32),
            vmem((units, width), f32),
            vmem((units, half), f32),
            vmem((units, half), f32),
            vmem((units, half), b16),
            dma((n,)), dma((n,)), dma((n,)), dma, dma,
            dma((n,)), dma((n,)), *[dma((tasks,))] * 4,
            dma((n,)), dma((n,)), dma((n,)), dma((n,)),
            dma((n,)), dma((n,)), dma, dma, dma((6,)), dma((3, n)),
        ],
        compiler_params=pltpu.CompilerParams(
            collective_id=0, has_side_effects=True, vmem_limit_bytes=56 * 2**20
        ),
        cost_estimate=pl.CostEstimate(
            flops=2 * tokens * width * features, bytes_accessed=24 * 2**20, transcendentals=0
        ),
    )(
        acts, out_grads, local_weight[0], adam_mean[0], adam_var[0],
        global_weight, outer_momentum, step_count,
    )


def solution(mesh):
    placed = (
        P(("worker", "shard"), None),
        P(("worker", "shard"), None),
        P("worker", "shard", None),
        P("worker", "shard", None),
        P("worker", "shard", None),
        P("shard", "worker"),
        P("shard", "worker"),
        P(),
    )
    grid = (2, CORES * ROWS_Y * LAYERS_Z)
    return jax.shard_map(
        fused if (mesh.shape["worker"], mesh.shape["shard"]) == grid else plain,
        mesh=mesh,
        in_specs=placed,
        out_specs=(P("shard", None), P("shard", "worker"), P("shard", "worker")),
        check_vma=False,
    )
```

```python
import functools
import math

import jax
import jax.numpy as jnp
from jax import lax
from jax.experimental import pallas as pl
from jax.experimental.pallas import tpu as pltpu
from jax.sharding import PartitionSpec as P

CORES = 2
ROWS_Y = 2
LAYERS_Z = 4
CHUNKS = 16
ZFIRST = 3
AHEAD = 3
LAG_Y = 2
LAG_Z = 5
LAG_DONE = 10


def inner_step(weight, mean, var, grad, count):
    moment = 0.9 * mean + 0.1 * grad
    second = 0.95 * var + 0.05 * grad * grad
    first_fix = 1.0 - jnp.power(0.9, count)
    second_fix = 1.0 - jnp.power(0.95, count)
    ratio = moment / first_fix / (jnp.sqrt(second / second_fix) + 1e-08)
    return weight - 0.1 * (ratio + 0.1 * weight)


def plain(
    acts, out_grads, local_weight, adam_mean, adam_var, global_weight, outer_momentum, step_count
):
    shards = lax.axis_size("shard")
    workers = lax.axis_size("worker")
    factor = 1.0 / math.sqrt(acts.shape[0] * shards)
    count = step_count[0].astype(jnp.float32)
    term = lax.dot_general(
        out_grads, acts, (((0,), (0,)), ((), ())), preferred_element_type=jnp.float32
    )
    grad = lax.psum_scatter(
        (term * factor).astype(jnp.bfloat16), "shard", scatter_dimension=0, tiled=True
    ).astype(jnp.float32)
    weight = local_weight[0].astype(jnp.float32)
    stepped = inner_step(weight, adam_mean[0], adam_var[0], grad, count)
    summed = lax.psum_scatter(stepped, "worker", scatter_dimension=1, tiled=True)
    delta = global_weight - summed / workers
    momentum = 0.9 * outer_momentum + delta
    updated = global_weight - 0.7 * (delta + 0.9 * momentum)
    synced = lax.all_gather(updated.astype(jnp.bfloat16), "worker", axis=1, tiled=True)
    return (synced, updated, momentum)


def kernel(
    factor, acts, grads, weight, mean, var, glob, outer, count,
    synced, new_glob, new_mom,
    a, g, gt, p, yin, ybin, lin, rin_z, gbuf, rout, rin, acc, ng, nm, sy, wv, mv, vv, gv, ov, wo,
    a_loc, a_out, a_in, gt_out, gt_in, y_out, y_in, rz_out, rz_in, lz_out, lz_in, c_out, c_in, r_out, r_in,
    s_out, s_in, w_out, w_in, loads, stores,
):
    r = lax.axis_index("worker")
    s = lax.axis_index("shard")
    z = lax.div(s, 4)
    y = lax.rem(lax.div(s, 2), 2)
    k = lax.rem(s, 2)
    tokens = acts.shape[0]
    chunks, _, cols = a.shape
    half = chunks * cols
    rows = yin.shape[1]
    units = gbuf.shape[2]
    block = CORES * units
    other_core = (r, z * 4 + y * 2 + 1 - k)
    other_y = (r, z * 4 + (1 - y) * 2 + k)
    other_worker = (1 - r, s)
    firsts = chunks - yin.shape[0]
    plains = chunks - firsts

    def remote(src, dst, send, recv, to):
        return pltpu.make_async_remote_copy(
            src_ref=src, dst_ref=dst, send_sem=send, recv_sem=recv,
            device_id=to, device_id_type=pl.DeviceIdType.MESH,
        )

    def at(start, step=cols):
        return pl.ds(pl.multiple_of(start, step), step)

    def acts_local(c):
        return pltpu.make_async_copy(
            acts.at[:, at(k * half + c * cols)], a.at[c, pl.ds(0, tokens)], a_loc.at[c]
        )

    def acts_remote(c):
        return remote(
            acts.at[:, at((1 - k) * half + c * cols)], a.at[c, pl.ds(tokens, tokens)],
            a_out.at[c], a_in.at[c], other_core,
        )

    def y_copy(c):
        return remote(
            p.at[c, at((1 - y) * rows, rows)], yin.at[c], y_out.at[c], y_in.at[c], other_y
        )

    def late_y_copy(c):
        return remote(
            p.at[c, at((1 - y) * rows + z * block, block)], ybin.at[c - plains],
            y_out.at[c], y_in.at[c], other_y,
        )

    def right_copy(task, c, part, here, t):
        return remote(
            p.at[c, at(part * rows + t * block, block)], rin_z.at[task, t - 1],
            rz_out.at[task, t - 1], rz_in.at[task, t - 1], (r, (here + 1) * 4 + y * 2 + k),
        )

    def left_copy(task, c, part, here, t):
        return remote(
            p.at[c, at(part * rows + t * block, block)], lin.at[task, t],
            lz_out.at[task, t], lz_in.at[task, t], (r, (here - 1) * 4 + y * 2 + k),
        )

    def add_to(c, part, low, high, *arrived):
        where = pl.ds(pl.multiple_of(part * rows + low * block, block), (high - low) * block)
        value = p[c, where].astype(jnp.float32)
        for ref in arrived:
            value += ref.astype(jnp.float32)
        p[c, where] = value.astype(jnp.bfloat16)

    def pass_right(task, c, part, here, t):
        right_copy(task, c, part, here - 1, t).wait_recv()
        add_to(c, part, t, t + 1, rin_z[task, t - 1])
        right_copy(task, c, part, here, t).start()

    def pass_left(task, c, part, here, t):
        left_copy(task, c, part, here + 1, t).wait_recv()
        add_to(c, part, t, t + 1, lin[task, t])
        left_copy(task, c, part, here, t).start()

    def line_start(task, c, part):
        @pl.when(z == 0)
        def _():
            for t in (3, 2, 1):
                right_copy(task, c, part, 0, t).start()

        @pl.when(z == 3)
        def _():
            for t in (0, 1, 2):
                left_copy(task, c, part, 3, t).start()

    def line_inward(task, c, part):
        @pl.when(z == 1)
        def _():
            for t in (3, 2):
                pass_right(task, c, part, 1, t)

        @pl.when(z == 2)
        def _():
            for t in (0, 1):
                pass_left(task, c, part, 2, t)

    def line_outward(task, c, part):
        @pl.when(z == 1)
        def _():
            pass_left(task, c, part, 1, 0)

        @pl.when(z == 2)
        def _():
            pass_right(task, c, part, 2, 3)

    def line_end(task, c, part):
        for here in range(LAYERS_Z):

            @pl.when(z == here)
            def _(here=here):
                arrived = []
                if here > 0:
                    right_copy(task, c, part, here - 1, here).wait_recv()
                    arrived.append(rin_z[task, here - 1])
                if here < LAYERS_Z - 1:
                    left_copy(task, c, part, here + 1, here).wait_recv()
                    arrived.append(lin[task, here])
                add_to(c, part, here, here + 1, *arrived)

    def line_sent(task, c, part):
        for here in range(LAYERS_Z):

            @pl.when(z == here)
            def _(here=here):
                for t in range(LAYERS_Z):
                    if t > here:
                        right_copy(task, c, part, here, t).wait_send()
                    if t < here:
                        left_copy(task, c, part, here, t).wait_send()

    def core_copy(c):
        return remote(
            p.at[c, at(y * rows + z * block + (1 - k) * units, units)], gbuf.at[c, k],
            c_out.at[c], c_in.at[c], other_core,
        )

    def ratio_copy(c):
        return remote(rout.at[c], rin.at[c], r_out.at[c], r_in.at[c], other_worker)

    def synced_copy(c):
        return remote(
            sy.at[c], synced.at[:, at(r * half + c * cols)], s_out.at[c], s_in.at[c], other_worker
        )

    def stores_of(c):
        return [
            pltpu.make_async_copy(sy.at[c], synced.at[:, at(r * half + c * cols)], stores.at[0, c]),
            pltpu.make_async_copy(ng.at[c], new_glob.at[:, at(c * cols)], stores.at[1, c]),
            pltpu.make_async_copy(nm.at[c], new_mom.at[:, at(c * cols)], stores.at[2, c]),
        ]

    grads_in = pltpu.make_async_copy(grads, g, loads.at[0])
    grads_in.start()

    @pl.loop(0, AHEAD)
    def _(c):
        acts_local(c).start()

    @pl.loop(0, firsts)
    def _(c):
        acts_local(plains + c).start()

    others = [
        pltpu.make_async_copy(x, v, loads.at[1 + j])
        for j, (x, v) in enumerate(
            ((weight, wv), (mean, mv), (var, vv), (glob, gv), (outer, ov))
        )
    ]
    barrier = pltpu.get_barrier_semaphore()
    for peer in (other_core, other_y, other_worker):
        pl.semaphore_signal(barrier, inc=1, device_id=peer, device_id_type=pl.DeviceIdType.MESH)

    @pl.when(z > 0)
    def _():
        pl.semaphore_signal(
            barrier, inc=1, device_id=(r, s - 4), device_id_type=pl.DeviceIdType.MESH
        )

    @pl.when(z < 3)
    def _():
        pl.semaphore_signal(
            barrier, inc=1, device_id=(r, s + 4), device_id_type=pl.DeviceIdType.MESH
        )

    grads_in.wait()
    for j in range(g.shape[1] // block):
        place = (j % ROWS_Y) * LAYERS_Z + j // ROWS_Y
        gt[place * block : (place + 1) * block, 0:tokens] = g[:, j * block : (j + 1) * block].T
    gt_copy = remote(
        gt.at[:, pl.ds(0, tokens)], gt.at[:, pl.ds(tokens, tokens)], gt_out, gt_in, other_core
    )
    weight_copy = remote(
        weight.at[:, at((1 - r) * half, half)], wo, w_out, w_in, other_worker
    )
    pl.semaphore_wait(barrier, 4 + lax.rem(lax.div(z + 1, 2), 2))
    gt_copy.start()

    acts_remote(0).start()
    acts_remote(1).start()
    acts_remote(plains).start()
    acts_remote(2).start()
    gt_copy.wait_recv()

    time = jnp.full((1, cols), count[0].astype(jnp.float32))
    first = 1.0 / (1.0 - jnp.exp(time * math.log(0.9)))
    second_inv = 1.0 / (1.0 - jnp.exp(time * math.log(0.95)))

    def ratio_of(c, side):
        where = at(side * half + c * cols)
        grad = gbuf[c, side].astype(jnp.float32) * factor
        moment = 0.9 * mv[:, where] + 0.1 * grad
        second = 0.95 * vv[:, where] + 0.05 * grad * grad
        return moment * first / (jnp.sqrt(second * second_inv) + 1e-08)

    def product(c, side):
        p[c, at(side * rows, rows)] = jnp.dot(
            gt[at(side * rows, rows)], a[c], preferred_element_type=jnp.float32
        ).astype(jnp.bfloat16)

    def fetched(c):
        acts_local(c).wait()
        acts_remote(c).wait_recv()

    def to_core(c):
        core_copy(c).start()
        gbuf[c, k] = p[c, at(y * rows + z * block + k * units, units)]

    def adam(c):
        core_copy(c).wait_recv()
        rout[c] = ratio_of(c, 1 - r).astype(jnp.bfloat16)
        ratio_copy(c).start()
        own = wv[:, at(r * half + c * cols)].astype(jnp.float32)
        acc[c] = own - 0.1 * (ratio_of(c, r) + 0.1 * own)

    def update(c):
        ratio_copy(c).wait_recv()
        where = at(c * cols)
        its = wo[:, where].astype(jnp.float32)
        summed = acc[c] + (its - 0.1 * (rin[c].astype(jnp.float32) + 0.1 * its))
        delta = gv[:, where] - summed * 0.5
        momentum = 0.9 * ov[:, where] + delta
        updated = gv[:, where] - 0.7 * (delta + 0.9 * momentum)
        sy[c] = updated.astype(jnp.bfloat16)
        synced_copy(c).start()
        ng[c] = updated
        nm[c] = momentum
        for copy in stores_of(c):
            copy.start()

    def done(c):
        acts_remote(c).wait_send()
        core_copy(c).wait_send()
        ratio_copy(c).wait_send()
        synced_copy(c).wait()
        for copy in stores_of(c):
            copy.wait()

    @pl.loop(0, plains + LAG_DONE)
    def _(i):
        def plain_at(lag):
            def run(stage):
                pl.when((i >= lag) & (i < plains + lag))(lambda: stage(i - lag))
            return run

        def first_at(lag):
            def run(stage):
                pl.when((i >= lag) & (i < firsts + lag))(lambda: stage(i - lag + plains))
            return run

        def halves(stage, c):
            for h in range(ROWS_Y):
                task = plains + (c - plains) * ROWS_Y + h
                stage(task, c, y if h == 1 else 1 - y)

        @plain_at(0)
        def _(c):
            fetched(c)
            product(c, 1 - y)
            y_copy(c).start()
            product(c, y)

        @pl.when(i + AHEAD < plains)
        def _():
            acts_local(i + AHEAD).start()
            acts_remote(i + AHEAD).start()

        @pl.when(i < firsts - 1)
        def _():
            acts_remote(plains + 1 + i).start()

        @first_at(1)
        def _(c):
            fetched(c)
            product(c, 1 - y)
            product(c, y)
            halves(line_start, c)

        @pl.when(i == 1)
        def _():
            weight_copy.start()
            for copy in others:
                copy.start()

        @first_at(plains)
        def _(c):
            late_y_copy(c).start()

        @plain_at(LAG_Y)
        def _(c):
            y_copy(c).wait_recv()
            add_to(c, y, 0, LAYERS_Z, yin[c])
            line_start(c, c, y)

        @first_at(plains + LAG_Y + 1)
        def _(c):
            late_y_copy(c).wait_recv()
            where = at(y * rows + z * block, block)
            p[c, where] = (
                p[c, where].astype(jnp.float32) + ybin[c - plains].astype(jnp.float32)
            ).astype(jnp.bfloat16)
            to_core(c)

        @first_at(plains + LAG_Y + 2)
        def _(c):
            adam(c)

        @first_at(plains + LAG_Y + 3)
        def _(c):
            update(c)

        @first_at(plains + LAG_Y + 4)
        def _(c):
            late_y_copy(c).wait_send()
            halves(line_sent, c)
            done(c)

        @first_at(4)
        def _(c):
            halves(line_inward, c)

        @plain_at(LAG_Z)
        def _(c):
            line_inward(c, c, y)

        @first_at(6)
        def _(c):
            halves(line_outward, c)

        @plain_at(LAG_Z + 1)
        def _(c):
            line_outward(c, c, y)

        @first_at(8)
        def _(c):
            halves(line_end, c)

        @plain_at(LAG_Z + 2)
        def _(c):
            line_end(c, c, y)
            to_core(c)

        @pl.when(i == LAG_Z + 3)
        def _():
            for copy in others:
                copy.wait()
            weight_copy.wait()

        @plain_at(LAG_Z + 3)
        def _(c):
            adam(c)

        @plain_at(LAG_Z + 4)
        def _(c):
            update(c)

        @plain_at(LAG_DONE)
        def _(c):
            y_copy(c).wait_send()
            line_sent(c, c, y)
            done(c)

    gt_copy.wait_send()


def place(a, b, c, to_a, to_b, to_c, sems):
    copies = [
        pltpu.make_async_copy(x, to, sems.at[j])
        for j, (x, to) in enumerate(((a, to_a), (b, to_b), (c, to_c)))
    ]
    for copy in copies:
        copy.start()
    for copy in copies:
        copy.wait()


def fused(
    acts, out_grads, local_weight, adam_mean, adam_var, global_weight, outer_momentum, step_count
):
    tokens, width = acts.shape
    features = out_grads.shape[1]
    units = local_weight.shape[1]
    half = width // CORES
    cols = half // CHUNKS
    rows = features // ROWS_Y
    factor = 1.0 / math.sqrt(tokens * lax.axis_size("shard"))
    b16, f32 = jnp.bfloat16, jnp.float32
    vmem, dma = pltpu.VMEM, pltpu.SemaphoreType.DMA
    n = CHUNKS
    tasks = n + ZFIRST * (ROWS_Y - 1)
    shapes = (
        jax.ShapeDtypeStruct((units, width), b16),
        jax.ShapeDtypeStruct((units, half), f32),
        jax.ShapeDtypeStruct((units, half), f32),
    )
    results = pl.pallas_call(
        functools.partial(kernel, factor),
        out_shape=shapes,
        in_specs=[pl.BlockSpec(memory_space=pl.ANY)] * 7
        + [pl.BlockSpec(memory_space=pltpu.SMEM)],
        out_specs=[pl.BlockSpec(memory_space=pl.ANY)] * 3,
        scratch_shapes=[
            vmem((n, CORES * tokens, cols), b16),
            vmem((tokens, features), b16),
            vmem((features, CORES * tokens), b16),
            vmem((n, features, cols), b16),
            vmem((n - ZFIRST, rows, cols), b16),
            vmem((ZFIRST, CORES * units, cols), b16),
            vmem((tasks, LAYERS_Z - 1, CORES * units, cols), b16),
            vmem((tasks, LAYERS_Z - 1, CORES * units, cols), b16),
            vmem((n, CORES, units, cols), b16),
            vmem((n, units, cols), b16),
            vmem((n, units, cols), b16),
            vmem((n, units, cols), f32),
            vmem((n, units, cols), f32),
            vmem((n, units, cols), f32),
            vmem((n, units, cols), b16),
            vmem((units, width), b16),
            vmem((units, width), f32),
            vmem((units, width), f32),
            vmem((units, half), f32),
            vmem((units, half), f32),
            vmem((units, half), b16),
            dma((n,)), dma((n,)), dma((n,)), dma, dma,
            dma((n,)), dma((n,)), *[dma((tasks, LAYERS_Z - 1))] * 4,
            dma((n,)), dma((n,)), dma((n,)), dma((n,)),
            dma((n,)), dma((n,)), dma, dma, dma((6,)), dma((3, n)),
        ],
        compiler_params=pltpu.CompilerParams(
            collective_id=0, has_side_effects=True, vmem_limit_bytes=56 * 2**20
        ),
        cost_estimate=pl.CostEstimate(
            flops=2 * tokens * width * features, bytes_accessed=24 * 2**20, transcendentals=0
        ),
    )(
        acts, out_grads, local_weight[0], adam_mean[0], adam_var[0],
        global_weight, outer_momentum, step_count,
    )
    return pl.pallas_call(
        place,
        out_shape=shapes,
        in_specs=[pl.BlockSpec(memory_space=pl.ANY)] * 3,
        out_specs=[pl.BlockSpec(memory_space=pl.ANY)] * 3,
        scratch_shapes=[dma((3,))],
        compiler_params=pltpu.CompilerParams(vmem_limit_bytes=56 * 2**20),
    )(*results)


def solution(mesh):
    placed = (
        P(("worker", "shard"), None),
        P(("worker", "shard"), None),
        P("worker", "shard", None),
        P("worker", "shard", None),
        P("worker", "shard", None),
        P("shard", "worker"),
        P("shard", "worker"),
        P(),
    )
    grid = (2, CORES * ROWS_Y * LAYERS_Z)
    return jax.shard_map(
        fused if (mesh.shape["worker"], mesh.shape["shard"]) == grid else plain,
        mesh=mesh,
        in_specs=placed,
        out_specs=(P("shard", None), P("shard", "worker"), P("shard", "worker")),
        check_vma=False,
    )
```

```python
import functools
import math

import jax
import jax.numpy as jnp
from jax import lax
from jax.experimental import pallas as pl
from jax.experimental.pallas import tpu as pltpu
from jax.sharding import PartitionSpec as P

CORES = 2
ROWS_Y = 2
LAYERS_Z = 4
CHUNKS = 16
ZFIRST = 3
AHEAD = 3
LAG_Y = 2
LAG_Z = 5
LAG_DONE = 10


def inner_step(weight, mean, var, grad, count):
    moment = 0.9 * mean + 0.1 * grad
    second = 0.95 * var + 0.05 * grad * grad
    first_fix = 1.0 - jnp.power(0.9, count)
    second_fix = 1.0 - jnp.power(0.95, count)
    ratio = moment / first_fix / (jnp.sqrt(second / second_fix) + 1e-08)
    return weight - 0.1 * (ratio + 0.1 * weight)


def plain(
    acts, out_grads, local_weight, adam_mean, adam_var, global_weight, outer_momentum, step_count
):
    shards = lax.axis_size("shard")
    workers = lax.axis_size("worker")
    factor = 1.0 / math.sqrt(acts.shape[0] * shards)
    count = step_count[0].astype(jnp.float32)
    term = lax.dot_general(
        out_grads, acts, (((0,), (0,)), ((), ())), preferred_element_type=jnp.float32
    )
    grad = lax.psum_scatter(
        (term * factor).astype(jnp.bfloat16), "shard", scatter_dimension=0, tiled=True
    ).astype(jnp.float32)
    weight = local_weight[0].astype(jnp.float32)
    stepped = inner_step(weight, adam_mean[0], adam_var[0], grad, count)
    summed = lax.psum_scatter(stepped, "worker", scatter_dimension=1, tiled=True)
    delta = global_weight - summed / workers
    momentum = 0.9 * outer_momentum + delta
    updated = global_weight - 0.7 * (delta + 0.9 * momentum)
    synced = lax.all_gather(updated.astype(jnp.bfloat16), "worker", axis=1, tiled=True)
    return (synced, updated, momentum)


def kernel(
    factor, acts, grads, weight, mean, var, glob, outer, count,
    synced, new_glob, new_mom,
    a, stage, g, gt, p, yin, ybin, lin, rin_z, gbuf, rout, rin, acc, ng, nm, sy, wv, mv, vv, gv, ov, wo,
    a_loc, st_loc, a_out, a_in, gt_out, gt_in, y_out, y_in, rz_out, rz_in, lz_out, lz_in, c_out, c_in, r_out, r_in,
    s_out, s_in, w_out, w_in, loads, stores,
):
    r = lax.axis_index("worker")
    s = lax.axis_index("shard")
    z = lax.div(s, 4)
    y = lax.rem(lax.div(s, 2), 2)
    k = lax.rem(s, 2)
    tokens = acts.shape[0]
    chunks, _, cols = a.shape
    half = chunks * cols
    rows = yin.shape[1]
    units = gbuf.shape[2]
    block = CORES * units
    other_core = (r, z * 4 + y * 2 + 1 - k)
    other_y = (r, z * 4 + (1 - y) * 2 + k)
    other_worker = (1 - r, s)
    firsts = chunks - yin.shape[0]
    plains = chunks - firsts

    def remote(src, dst, send, recv, to):
        return pltpu.make_async_remote_copy(
            src_ref=src, dst_ref=dst, send_sem=send, recv_sem=recv,
            device_id=to, device_id_type=pl.DeviceIdType.MESH,
        )

    def at(start, step=cols):
        return pl.ds(pl.multiple_of(start, step), step)

    def acts_local(c):
        return pltpu.make_async_copy(
            acts.at[:, at(k * half + c * cols)], a.at[c, pl.ds(0, tokens)], a_loc.at[c]
        )

    def acts_staged(c):
        return pltpu.make_async_copy(
            acts.at[:, at((1 - k) * half + c * cols)], stage.at[c], st_loc.at[c]
        )

    def acts_remote(c):
        return remote(
            stage.at[c], a.at[c, pl.ds(tokens, tokens)], a_out.at[c], a_in.at[c], other_core
        )

    def load_acts(c):
        acts_staged(c).start()
        acts_local(c).start()

    def send_acts(c):
        acts_staged(c).wait()
        acts_remote(c).start()

    def y_copy(c):
        return remote(
            p.at[c, at((1 - y) * rows, rows)], yin.at[c], y_out.at[c], y_in.at[c], other_y
        )

    def late_y_copy(c):
        return remote(
            p.at[c, at((1 - y) * rows + z * block, block)], ybin.at[c - plains],
            y_out.at[c], y_in.at[c], other_y,
        )

    def right_copy(task, c, part, here, t):
        return remote(
            p.at[c, at(part * rows + t * block, block)], rin_z.at[task, t - 1],
            rz_out.at[task, t - 1], rz_in.at[task, t - 1], (r, (here + 1) * 4 + y * 2 + k),
        )

    def left_copy(task, c, part, here, t):
        return remote(
            p.at[c, at(part * rows + t * block, block)], lin.at[task, t],
            lz_out.at[task, t], lz_in.at[task, t], (r, (here - 1) * 4 + y * 2 + k),
        )

    def add_to(c, part, low, high, *arrived):
        where = pl.ds(pl.multiple_of(part * rows + low * block, block), (high - low) * block)
        value = p[c, where].astype(jnp.float32)
        for ref in arrived:
            value += ref.astype(jnp.float32)
        p[c, where] = value.astype(jnp.bfloat16)

    def pass_right(task, c, part, here, t):
        right_copy(task, c, part, here - 1, t).wait_recv()
        add_to(c, part, t, t + 1, rin_z[task, t - 1])
        right_copy(task, c, part, here, t).start()

    def pass_left(task, c, part, here, t):
        left_copy(task, c, part, here + 1, t).wait_recv()
        add_to(c, part, t, t + 1, lin[task, t])
        left_copy(task, c, part, here, t).start()

    def line_start(task, c, part):
        @pl.when(z == 0)
        def _():
            for t in (3, 2, 1):
                right_copy(task, c, part, 0, t).start()

        @pl.when(z == 3)
        def _():
            for t in (0, 1, 2):
                left_copy(task, c, part, 3, t).start()

    def line_inward(task, c, part):
        @pl.when(z == 1)
        def _():
            for t in (3, 2):
                pass_right(task, c, part, 1, t)

        @pl.when(z == 2)
        def _():
            for t in (0, 1):
                pass_left(task, c, part, 2, t)

    def line_outward(task, c, part):
        @pl.when(z == 1)
        def _():
            pass_left(task, c, part, 1, 0)

        @pl.when(z == 2)
        def _():
            pass_right(task, c, part, 2, 3)

    def line_end(task, c, part):
        for here in range(LAYERS_Z):

            @pl.when(z == here)
            def _(here=here):
                arrived = []
                if here > 0:
                    right_copy(task, c, part, here - 1, here).wait_recv()
                    arrived.append(rin_z[task, here - 1])
                if here < LAYERS_Z - 1:
                    left_copy(task, c, part, here + 1, here).wait_recv()
                    arrived.append(lin[task, here])
                add_to(c, part, here, here + 1, *arrived)

    def line_sent(task, c, part):
        for here in range(LAYERS_Z):

            @pl.when(z == here)
            def _(here=here):
                for t in range(LAYERS_Z):
                    if t > here:
                        right_copy(task, c, part, here, t).wait_send()
                    if t < here:
                        left_copy(task, c, part, here, t).wait_send()

    def core_copy(c):
        return remote(
            p.at[c, at(y * rows + z * block + (1 - k) * units, units)], gbuf.at[c, k],
            c_out.at[c], c_in.at[c], other_core,
        )

    def ratio_copy(c):
        return remote(rout.at[c], rin.at[c], r_out.at[c], r_in.at[c], other_worker)

    def synced_copy(c):
        return remote(
            sy.at[c], synced.at[:, at(r * half + c * cols)], s_out.at[c], s_in.at[c], other_worker
        )

    def stores_of(c):
        return [
            pltpu.make_async_copy(sy.at[c], synced.at[:, at(r * half + c * cols)], stores.at[0, c]),
            pltpu.make_async_copy(ng.at[c], new_glob.at[:, at(c * cols)], stores.at[1, c]),
            pltpu.make_async_copy(nm.at[c], new_mom.at[:, at(c * cols)], stores.at[2, c]),
        ]

    grads_in = pltpu.make_async_copy(grads, g, loads.at[0])
    grads_in.start()

    load_acts(0)
    load_acts(1)
    load_acts(plains)

    others = [
        pltpu.make_async_copy(x, v, loads.at[1 + j])
        for j, (x, v) in enumerate(
            ((weight, wv), (mean, mv), (var, vv), (glob, gv), (outer, ov))
        )
    ]
    barrier = pltpu.get_barrier_semaphore()
    for peer in (other_core, other_y, other_worker):
        pl.semaphore_signal(barrier, inc=1, device_id=peer, device_id_type=pl.DeviceIdType.MESH)

    @pl.when(z > 0)
    def _():
        pl.semaphore_signal(
            barrier, inc=1, device_id=(r, s - 4), device_id_type=pl.DeviceIdType.MESH
        )

    @pl.when(z < 3)
    def _():
        pl.semaphore_signal(
            barrier, inc=1, device_id=(r, s + 4), device_id_type=pl.DeviceIdType.MESH
        )

    grads_in.wait()
    for j in range(g.shape[1] // block):
        place = (j % ROWS_Y) * LAYERS_Z + j // ROWS_Y
        gt[place * block : (place + 1) * block, 0:tokens] = g[:, j * block : (j + 1) * block].T
    gt_copy = remote(
        gt.at[:, pl.ds(0, tokens)], gt.at[:, pl.ds(tokens, tokens)], gt_out, gt_in, other_core
    )
    weight_copy = remote(
        wv.at[:, at((1 - r) * half, half)], wo, w_out, w_in, other_worker
    )
    pl.semaphore_wait(barrier, 4 + lax.rem(lax.div(z + 1, 2), 2))
    gt_copy.start()

    send_acts(0)
    send_acts(1)
    send_acts(plains)

    @pl.loop(2, plains)
    def _(c):
        load_acts(c)

    @pl.loop(plains + 1, chunks)
    def _(c):
        load_acts(c)

    send_acts(2)
    gt_copy.wait_recv()

    time = jnp.full((1, cols), count[0].astype(jnp.float32))
    first = 1.0 / (1.0 - jnp.exp(time * math.log(0.9)))
    second_inv = 1.0 / (1.0 - jnp.exp(time * math.log(0.95)))

    def ratio_of(c, side):
        where = at(side * half + c * cols)
        grad = gbuf[c, side].astype(jnp.float32) * factor
        moment = 0.9 * mv[:, where] + 0.1 * grad
        second = 0.95 * vv[:, where] + 0.05 * grad * grad
        return moment * first / (jnp.sqrt(second * second_inv) + 1e-08)

    def product(c, side):
        p[c, at(side * rows, rows)] = jnp.dot(
            gt[at(side * rows, rows)], a[c], preferred_element_type=jnp.float32
        ).astype(jnp.bfloat16)

    def fetched(c):
        acts_local(c).wait()
        acts_remote(c).wait_recv()

    def to_core(c):
        core_copy(c).start()
        gbuf[c, k] = p[c, at(y * rows + z * block + k * units, units)]

    def adam(c):
        core_copy(c).wait_recv()
        rout[c] = ratio_of(c, 1 - r).astype(jnp.bfloat16)
        ratio_copy(c).start()
        own = wv[:, at(r * half + c * cols)].astype(jnp.float32)
        acc[c] = own - 0.1 * (ratio_of(c, r) + 0.1 * own)

    def update(c):
        ratio_copy(c).wait_recv()
        where = at(c * cols)
        its = wo[:, where].astype(jnp.float32)
        summed = acc[c] + (its - 0.1 * (rin[c].astype(jnp.float32) + 0.1 * its))
        delta = gv[:, where] - summed * 0.5
        momentum = 0.9 * ov[:, where] + delta
        updated = gv[:, where] - 0.7 * (delta + 0.9 * momentum)
        sy[c] = updated.astype(jnp.bfloat16)
        synced_copy(c).start()
        ng[c] = updated
        nm[c] = momentum
        for copy in stores_of(c):
            copy.start()

    def done(c):
        acts_remote(c).wait_send()
        core_copy(c).wait_send()
        ratio_copy(c).wait_send()
        synced_copy(c).wait()
        for copy in stores_of(c):
            copy.wait()

    @pl.loop(0, plains + LAG_DONE)
    def _(i):
        def plain_at(lag):
            def run(stage):
                pl.when((i >= lag) & (i < plains + lag))(lambda: stage(i - lag))
            return run

        def first_at(lag):
            def run(stage):
                pl.when((i >= lag) & (i < firsts + lag))(lambda: stage(i - lag + plains))
            return run

        def halves(stage, c):
            for h in range(ROWS_Y):
                task = plains + (c - plains) * ROWS_Y + h
                stage(task, c, y if h == 1 else 1 - y)

        @plain_at(0)
        def _(c):
            fetched(c)
            product(c, 1 - y)
            y_copy(c).start()
            product(c, y)

        @pl.when(i + AHEAD < plains)
        def _():
            send_acts(i + AHEAD)

        @pl.when(i < firsts - 1)
        def _():
            send_acts(plains + 1 + i)

        @first_at(1)
        def _(c):
            fetched(c)
            product(c, 1 - y)
            product(c, y)
            halves(line_start, c)

        @pl.when(i == 1)
        def _():
            for copy in others:
                copy.start()

        @pl.when(i == 3)
        def _():
            for copy in others:
                copy.wait()
            weight_copy.start()

        @first_at(plains)
        def _(c):
            late_y_copy(c).start()

        @plain_at(LAG_Y)
        def _(c):
            y_copy(c).wait_recv()
            add_to(c, y, 0, LAYERS_Z, yin[c])
            line_start(c, c, y)

        @first_at(plains + LAG_Y + 1)
        def _(c):
            late_y_copy(c).wait_recv()
            where = at(y * rows + z * block, block)
            p[c, where] = (
                p[c, where].astype(jnp.float32) + ybin[c - plains].astype(jnp.float32)
            ).astype(jnp.bfloat16)
            to_core(c)

        @first_at(plains + LAG_Y + 2)
        def _(c):
            adam(c)

        @first_at(plains + LAG_Y + 3)
        def _(c):
            update(c)

        @first_at(plains + LAG_Y + 4)
        def _(c):
            late_y_copy(c).wait_send()
            halves(line_sent, c)
            done(c)

        @first_at(4)
        def _(c):
            halves(line_inward, c)

        @plain_at(LAG_Z)
        def _(c):
            line_inward(c, c, y)

        @first_at(6)
        def _(c):
            halves(line_outward, c)

        @plain_at(LAG_Z + 1)
        def _(c):
            line_outward(c, c, y)

        @first_at(8)
        def _(c):
            halves(line_end, c)

        @plain_at(LAG_Z + 2)
        def _(c):
            line_end(c, c, y)
            to_core(c)

        @pl.when(i == LAG_Z + 3)
        def _():
            weight_copy.wait()

        @plain_at(LAG_Z + 3)
        def _(c):
            adam(c)

        @plain_at(LAG_Z + 4)
        def _(c):
            update(c)

        @plain_at(LAG_DONE)
        def _(c):
            y_copy(c).wait_send()
            line_sent(c, c, y)
            done(c)

    gt_copy.wait_send()


def place(a, b, c, to_a, to_b, to_c, held_a, held_b, held_c, sems, out_sems):
    pieces = 2
    loads, stores = [], []
    for p in range(pieces):
        for j, (x, held, to) in enumerate(
            ((a, held_a, to_a), (b, held_b, to_b), (c, held_c, to_c))
        ):
            size = x.shape[0] // pieces
            rows = pl.ds(p * size, size)
            loads.append(pltpu.make_async_copy(x.at[rows], held.at[rows], sems.at[p, j]))
            stores.append(pltpu.make_async_copy(held.at[rows], to.at[rows], out_sems.at[p, j]))
    for copy in loads:
        copy.start()
    for load, store in zip(loads, stores):
        load.wait()
        store.start()
    for copy in stores:
        copy.wait()


def fused(
    acts, out_grads, local_weight, adam_mean, adam_var, global_weight, outer_momentum, step_count
):
    tokens, width = acts.shape
    features = out_grads.shape[1]
    units = local_weight.shape[1]
    half = width // CORES
    cols = half // CHUNKS
    rows = features // ROWS_Y
    factor = 1.0 / math.sqrt(tokens * lax.axis_size("shard"))
    b16, f32 = jnp.bfloat16, jnp.float32
    vmem, dma = pltpu.VMEM, pltpu.SemaphoreType.DMA
    n = CHUNKS
    tasks = n + ZFIRST * (ROWS_Y - 1)
    shapes = (
        jax.ShapeDtypeStruct((units, width), b16),
        jax.ShapeDtypeStruct((units, half), f32),
        jax.ShapeDtypeStruct((units, half), f32),
    )
    results = pl.pallas_call(
        functools.partial(kernel, factor),
        out_shape=shapes,
        in_specs=[pl.BlockSpec(memory_space=pl.ANY)] * 7
        + [pl.BlockSpec(memory_space=pltpu.SMEM)],
        out_specs=[pl.BlockSpec(memory_space=pl.ANY)] * 3,
        scratch_shapes=[
            vmem((n, CORES * tokens, cols), b16),
            vmem((n, tokens, cols), b16),
            vmem((tokens, features), b16),
            vmem((features, CORES * tokens), b16),
            vmem((n, features, cols), b16),
            vmem((n - ZFIRST, rows, cols), b16),
            vmem((ZFIRST, CORES * units, cols), b16),
            vmem((tasks, LAYERS_Z - 1, CORES * units, cols), b16),
            vmem((tasks, LAYERS_Z - 1, CORES * units, cols), b16),
            vmem((n, CORES, units, cols), b16),
            vmem((n, units, cols), b16),
            vmem((n, units, cols), b16),
            vmem((n, units, cols), f32),
            vmem((n, units, cols), f32),
            vmem((n, units, cols), f32),
            vmem((n, units, cols), b16),
            vmem((units, width), b16),
            vmem((units, width), f32),
            vmem((units, width), f32),
            vmem((units, half), f32),
            vmem((units, half), f32),
            vmem((units, half), b16),
            dma((n,)), dma((n,)), dma((n,)), dma((n,)), dma, dma,
            dma((n,)), dma((n,)), *[dma((tasks, LAYERS_Z - 1))] * 4,
            dma((n,)), dma((n,)), dma((n,)), dma((n,)),
            dma((n,)), dma((n,)), dma, dma, dma((6,)), dma((3, n)),
        ],
        compiler_params=pltpu.CompilerParams(
            collective_id=0, has_side_effects=True, vmem_limit_bytes=56 * 2**20
        ),
        cost_estimate=pl.CostEstimate(
            flops=2 * tokens * width * features, bytes_accessed=24 * 2**20, transcendentals=0
        ),
    )(
        acts, out_grads, local_weight[0], adam_mean[0], adam_var[0],
        global_weight, outer_momentum, step_count,
    )
    return pl.pallas_call(
        place,
        out_shape=shapes,
        in_specs=[pl.BlockSpec(memory_space=pl.ANY)] * 3,
        out_specs=[pl.BlockSpec(memory_space=pl.ANY)] * 3,
        scratch_shapes=[vmem(x.shape, x.dtype) for x in shapes] + [dma((2, 3)), dma((2, 3))],
        compiler_params=pltpu.CompilerParams(vmem_limit_bytes=56 * 2**20),
    )(*results)


def solution(mesh):
    placed = (
        P(("worker", "shard"), None),
        P(("worker", "shard"), None),
        P("worker", "shard", None),
        P("worker", "shard", None),
        P("worker", "shard", None),
        P("shard", "worker"),
        P("shard", "worker"),
        P(),
    )
    grid = (2, CORES * ROWS_Y * LAYERS_Z)
    return jax.shard_map(
        fused if (mesh.shape["worker"], mesh.shape["shard"]) == grid else plain,
        mesh=mesh,
        in_specs=placed,
        out_specs=(P("shard", None), P("shard", "worker"), P("shard", "worker")),
        check_vma=False,
    )
```

```python
import functools
import math

import jax
import jax.numpy as jnp
from jax import lax
from jax.experimental import pallas as pl
from jax.experimental.pallas import tpu as pltpu
from jax.sharding import PartitionSpec as P

CORES = 2
ROWS_Y = 2
LAYERS_Z = 4
CHUNKS = 16
ZFIRST = 3
AHEAD = 3
LAG_Y = 2
LAG_Z = 5
LAG_DONE = 10


def inner_step(weight, mean, var, grad, count):
    moment = 0.9 * mean + 0.1 * grad
    second = 0.95 * var + 0.05 * grad * grad
    first_fix = 1.0 - jnp.power(0.9, count)
    second_fix = 1.0 - jnp.power(0.95, count)
    ratio = moment / first_fix / (jnp.sqrt(second / second_fix) + 1e-08)
    return weight - 0.1 * (ratio + 0.1 * weight)


def plain(
    acts, out_grads, local_weight, adam_mean, adam_var, global_weight, outer_momentum, step_count
):
    shards = lax.axis_size("shard")
    workers = lax.axis_size("worker")
    factor = 1.0 / math.sqrt(acts.shape[0] * shards)
    count = step_count[0].astype(jnp.float32)
    term = lax.dot_general(
        out_grads, acts, (((0,), (0,)), ((), ())), preferred_element_type=jnp.float32
    )
    grad = lax.psum_scatter(
        (term * factor).astype(jnp.bfloat16), "shard", scatter_dimension=0, tiled=True
    ).astype(jnp.float32)
    weight = local_weight[0].astype(jnp.float32)
    stepped = inner_step(weight, adam_mean[0], adam_var[0], grad, count)
    summed = lax.psum_scatter(stepped, "worker", scatter_dimension=1, tiled=True)
    delta = global_weight - summed / workers
    momentum = 0.9 * outer_momentum + delta
    updated = global_weight - 0.7 * (delta + 0.9 * momentum)
    synced = lax.all_gather(updated.astype(jnp.bfloat16), "worker", axis=1, tiled=True)
    return (synced, updated, momentum)


def kernel(
    factor, acts, grads, weight, mean, var, glob, outer, count,
    synced, new_glob, new_mom,
    a, stage, g, gt, p, yin, ybin, lin, rin_z, gbuf, rout, rin, acc, ng, nm, sy, wv, mv, vv, gv, ov, wo,
    a_loc, st_loc, a_out, a_in, gt_out, gt_in, y_out, y_in, rz_out, rz_in, lz_out, lz_in, c_out, c_in, r_out, r_in,
    s_out, s_in, w_out, w_in, loads, stores,
):
    r = lax.axis_index("worker")
    s = lax.axis_index("shard")
    z = lax.div(s, 4)
    y = lax.rem(lax.div(s, 2), 2)
    k = lax.rem(s, 2)
    tokens = acts.shape[0]
    chunks, _, cols = a.shape
    half = chunks * cols
    rows = yin.shape[1]
    units = gbuf.shape[2]
    block = CORES * units
    other_core = (r, z * 4 + y * 2 + 1 - k)
    other_y = (r, z * 4 + (1 - y) * 2 + k)
    other_worker = (1 - r, s)
    firsts = chunks - yin.shape[0]
    plains = chunks - firsts

    def remote(src, dst, send, recv, to):
        return pltpu.make_async_remote_copy(
            src_ref=src, dst_ref=dst, send_sem=send, recv_sem=recv,
            device_id=to, device_id_type=pl.DeviceIdType.MESH,
        )

    def at(start, step=cols):
        return pl.ds(pl.multiple_of(start, step), step)

    def acts_local(c):
        return pltpu.make_async_copy(
            acts.at[:, at(k * half + c * cols)], a.at[c, pl.ds(0, tokens)], a_loc.at[c]
        )

    def acts_staged(c):
        return pltpu.make_async_copy(
            acts.at[:, at((1 - k) * half + c * cols)], stage.at[c], st_loc.at[c]
        )

    def acts_remote(c):
        return remote(
            stage.at[c], a.at[c, pl.ds(tokens, tokens)], a_out.at[c], a_in.at[c], other_core
        )

    def load_acts(c):
        acts_staged(c).start()
        acts_local(c).start()

    def send_acts(c):
        acts_staged(c).wait()
        acts_remote(c).start()

    def y_copy(c):
        return remote(
            p.at[c, at((1 - y) * rows, rows)], yin.at[c], y_out.at[c], y_in.at[c], other_y
        )

    def late_y_copy(c):
        return remote(
            p.at[c, at((1 - y) * rows + z * block, block)], ybin.at[c - plains],
            y_out.at[c], y_in.at[c], other_y,
        )

    def right_copy(task, c, part, here, t):
        return remote(
            p.at[c, at(part * rows + t * block, block)], rin_z.at[task, t - 1],
            rz_out.at[task, t - 1], rz_in.at[task, t - 1], (r, (here + 1) * 4 + y * 2 + k),
        )

    def left_copy(task, c, part, here, t):
        return remote(
            p.at[c, at(part * rows + t * block, block)], lin.at[task, t],
            lz_out.at[task, t], lz_in.at[task, t], (r, (here - 1) * 4 + y * 2 + k),
        )

    def add_to(c, part, low, high, *arrived):
        where = pl.ds(pl.multiple_of(part * rows + low * block, block), (high - low) * block)
        value = p[c, where].astype(jnp.float32)
        for ref in arrived:
            value += ref.astype(jnp.float32)
        p[c, where] = value.astype(jnp.bfloat16)

    def pass_right(task, c, part, here, t):
        right_copy(task, c, part, here - 1, t).wait_recv()
        add_to(c, part, t, t + 1, rin_z[task, t - 1])
        right_copy(task, c, part, here, t).start()

    def pass_left(task, c, part, here, t):
        left_copy(task, c, part, here + 1, t).wait_recv()
        add_to(c, part, t, t + 1, lin[task, t])
        left_copy(task, c, part, here, t).start()

    def line_start(task, c, part):
        @pl.when(z == 0)
        def _():
            for t in (3, 2, 1):
                right_copy(task, c, part, 0, t).start()

        @pl.when(z == 3)
        def _():
            for t in (0, 1, 2):
                left_copy(task, c, part, 3, t).start()

    def line_inward(task, c, part):
        @pl.when(z == 1)
        def _():
            for t in (3, 2):
                pass_right(task, c, part, 1, t)

        @pl.when(z == 2)
        def _():
            for t in (0, 1):
                pass_left(task, c, part, 2, t)

    def line_outward(task, c, part):
        @pl.when(z == 1)
        def _():
            pass_left(task, c, part, 1, 0)

        @pl.when(z == 2)
        def _():
            pass_right(task, c, part, 2, 3)

    def line_end(task, c, part):
        for here in range(LAYERS_Z):

            @pl.when(z == here)
            def _(here=here):
                arrived = []
                if here > 0:
                    right_copy(task, c, part, here - 1, here).wait_recv()
                    arrived.append(rin_z[task, here - 1])
                if here < LAYERS_Z - 1:
                    left_copy(task, c, part, here + 1, here).wait_recv()
                    arrived.append(lin[task, here])
                add_to(c, part, here, here + 1, *arrived)

    def line_sent(task, c, part):
        for here in range(LAYERS_Z):

            @pl.when(z == here)
            def _(here=here):
                for t in range(LAYERS_Z):
                    if t > here:
                        right_copy(task, c, part, here, t).wait_send()
                    if t < here:
                        left_copy(task, c, part, here, t).wait_send()

    def core_copy(c):
        return remote(
            p.at[c, at(y * rows + z * block + (1 - k) * units, units)], gbuf.at[c, k],
            c_out.at[c], c_in.at[c], other_core,
        )

    def ratio_copy(c):
        return remote(rout.at[c], rin.at[c], r_out.at[c], r_in.at[c], other_worker)

    def synced_copy(c):
        return remote(
            sy.at[c], synced.at[:, at(r * half + c * cols)], s_out.at[c], s_in.at[c], other_worker
        )

    def stores_of(c):
        return [
            pltpu.make_async_copy(sy.at[c], synced.at[:, at(r * half + c * cols)], stores.at[0, c]),
            pltpu.make_async_copy(ng.at[c], new_glob.at[:, at(c * cols)], stores.at[1, c]),
            pltpu.make_async_copy(nm.at[c], new_mom.at[:, at(c * cols)], stores.at[2, c]),
        ]

    grads_in = pltpu.make_async_copy(grads, g, loads.at[0])
    grads_in.start()

    load_acts(0)
    load_acts(1)
    load_acts(plains)

    others = [
        pltpu.make_async_copy(x, v, loads.at[1 + j])
        for j, (x, v) in enumerate(
            ((weight, wv), (mean, mv), (var, vv), (glob, gv), (outer, ov))
        )
    ]
    barrier = pltpu.get_barrier_semaphore()
    for peer in (other_core, other_y, other_worker):
        pl.semaphore_signal(barrier, inc=1, device_id=peer, device_id_type=pl.DeviceIdType.MESH)

    @pl.when(z > 0)
    def _():
        pl.semaphore_signal(
            barrier, inc=1, device_id=(r, s - 4), device_id_type=pl.DeviceIdType.MESH
        )

    @pl.when(z < 3)
    def _():
        pl.semaphore_signal(
            barrier, inc=1, device_id=(r, s + 4), device_id_type=pl.DeviceIdType.MESH
        )

    grads_in.wait()
    for j in range(g.shape[1] // block):
        place = (j % ROWS_Y) * LAYERS_Z + j // ROWS_Y
        gt[place * block : (place + 1) * block, 0:tokens] = g[:, j * block : (j + 1) * block].T
    def gt_copy(side):
        where = at(side * rows, rows)
        return remote(
            gt.at[where, pl.ds(0, tokens)], gt.at[where, pl.ds(tokens, tokens)],
            gt_out.at[side], gt_in.at[side], other_core,
        )

    weight_copy = remote(
        wv.at[:, at((1 - r) * half, half)], wo, w_out, w_in, other_worker
    )
    pl.semaphore_wait(barrier, 4 + lax.rem(lax.div(z + 1, 2), 2))
    gt_copy(1 - y).start()

    send_acts(0)
    gt_copy(y).start()
    send_acts(plains)
    send_acts(1)

    @pl.loop(2, plains)
    def _(c):
        load_acts(c)

    @pl.loop(plains + 1, chunks)
    def _(c):
        load_acts(c)

    send_acts(2)
    gt_copy(1 - y).wait_recv()

    time = jnp.full((1, cols), count[0].astype(jnp.float32))
    first = 1.0 / (1.0 - jnp.exp(time * math.log(0.9)))
    second_inv = 1.0 / (1.0 - jnp.exp(time * math.log(0.95)))

    def ratio_of(c, side):
        where = at(side * half + c * cols)
        grad = gbuf[c, side].astype(jnp.float32) * factor
        moment = 0.9 * mv[:, where] + 0.1 * grad
        second = 0.95 * vv[:, where] + 0.05 * grad * grad
        return moment * first / (jnp.sqrt(second * second_inv) + 1e-08)

    def product(c, side):
        p[c, at(side * rows, rows)] = jnp.dot(
            gt[at(side * rows, rows)], a[c], preferred_element_type=jnp.float32
        ).astype(jnp.bfloat16)

    def fetched(c):
        acts_local(c).wait()
        acts_remote(c).wait_recv()

    def to_core(c):
        core_copy(c).start()
        gbuf[c, k] = p[c, at(y * rows + z * block + k * units, units)]

    def adam(c):
        core_copy(c).wait_recv()
        rout[c] = ratio_of(c, 1 - r).astype(jnp.bfloat16)
        ratio_copy(c).start()
        own = wv[:, at(r * half + c * cols)].astype(jnp.float32)
        acc[c] = own - 0.1 * (ratio_of(c, r) + 0.1 * own)

    def update(c):
        ratio_copy(c).wait_recv()
        where = at(c * cols)
        its = wo[:, where].astype(jnp.float32)
        summed = acc[c] + (its - 0.1 * (rin[c].astype(jnp.float32) + 0.1 * its))
        delta = gv[:, where] - summed * 0.5
        momentum = 0.9 * ov[:, where] + delta
        updated = gv[:, where] - 0.7 * (delta + 0.9 * momentum)
        sy[c] = updated.astype(jnp.bfloat16)
        synced_copy(c).start()
        ng[c] = updated
        nm[c] = momentum
        for copy in stores_of(c):
            copy.start()

    def done(c):
        acts_remote(c).wait_send()
        core_copy(c).wait_send()
        ratio_copy(c).wait_send()
        synced_copy(c).wait()
        for copy in stores_of(c):
            copy.wait()

    @pl.loop(0, plains + LAG_DONE)
    def _(i):
        def plain_at(lag):
            def run(stage):
                pl.when((i >= lag) & (i < plains + lag))(lambda: stage(i - lag))
            return run

        def first_at(lag):
            def run(stage):
                pl.when((i >= lag) & (i < firsts + lag))(lambda: stage(i - lag + plains))
            return run

        def halves(stage, c):
            for h in range(ROWS_Y):
                task = plains + (c - plains) * ROWS_Y + h
                stage(task, c, y if h == 1 else 1 - y)

        @plain_at(0)
        def _(c):
            fetched(c)
            product(c, 1 - y)
            y_copy(c).start()

        @pl.when(i == 0)
        def _():
            gt_copy(y).wait_recv()

        @first_at(0)
        def _(c):
            fetched(c)
            for h, part in enumerate((1 - y, y)):
                product(c, part)
                line_start(plains + (c - plains) * ROWS_Y + h, c, part)

        @plain_at(0)
        def _(c):
            product(c, y)

        @pl.when(i + AHEAD < plains)
        def _():
            send_acts(i + AHEAD)

        @pl.when(i < firsts - 1)
        def _():
            send_acts(plains + 1 + i)

        @pl.when(i == 1)
        def _():
            for copy in others:
                copy.start()

        @pl.when(i == 3)
        def _():
            for copy in others:
                copy.wait()
            weight_copy.start()

        @first_at(plains)
        def _(c):
            late_y_copy(c).start()

        @plain_at(LAG_Y)
        def _(c):
            y_copy(c).wait_recv()
            add_to(c, y, 0, LAYERS_Z, yin[c])
            line_start(c, c, y)

        @first_at(plains + LAG_Y + 1)
        def _(c):
            late_y_copy(c).wait_recv()
            where = at(y * rows + z * block, block)
            p[c, where] = (
                p[c, where].astype(jnp.float32) + ybin[c - plains].astype(jnp.float32)
            ).astype(jnp.bfloat16)
            to_core(c)

        @first_at(plains + LAG_Y + 2)
        def _(c):
            adam(c)

        @first_at(plains + LAG_Y + 3)
        def _(c):
            update(c)

        @first_at(plains + LAG_Y + 4)
        def _(c):
            late_y_copy(c).wait_send()
            halves(line_sent, c)
            done(c)

        @first_at(4)
        def _(c):
            halves(line_inward, c)

        @plain_at(LAG_Z)
        def _(c):
            line_inward(c, c, y)

        @first_at(6)
        def _(c):
            halves(line_outward, c)

        @plain_at(LAG_Z + 1)
        def _(c):
            line_outward(c, c, y)

        @first_at(8)
        def _(c):
            halves(line_end, c)

        @plain_at(LAG_Z + 2)
        def _(c):
            line_end(c, c, y)
            to_core(c)

        @pl.when(i == LAG_Z + 3)
        def _():
            weight_copy.wait()

        @plain_at(LAG_Z + 3)
        def _(c):
            adam(c)

        @plain_at(LAG_Z + 4)
        def _(c):
            update(c)

        @plain_at(LAG_DONE)
        def _(c):
            y_copy(c).wait_send()
            line_sent(c, c, y)
            done(c)

    gt_copy(0).wait_send()
    gt_copy(1).wait_send()


def place(a, b, c, to_a, to_b, to_c, held_a, held_b, held_c, sems, out_sems):
    pieces = 2
    loads, stores = [], []
    for p in range(pieces):
        for j, (x, held, to) in enumerate(
            ((a, held_a, to_a), (b, held_b, to_b), (c, held_c, to_c))
        ):
            size = x.shape[0] // pieces
            rows = pl.ds(p * size, size)
            loads.append(pltpu.make_async_copy(x.at[rows], held.at[rows], sems.at[p, j]))
            stores.append(pltpu.make_async_copy(held.at[rows], to.at[rows], out_sems.at[p, j]))
    for copy in loads:
        copy.start()
    for load, store in zip(loads, stores):
        load.wait()
        store.start()
    for copy in stores:
        copy.wait()


def fused(
    acts, out_grads, local_weight, adam_mean, adam_var, global_weight, outer_momentum, step_count
):
    tokens, width = acts.shape
    features = out_grads.shape[1]
    units = local_weight.shape[1]
    half = width // CORES
    cols = half // CHUNKS
    rows = features // ROWS_Y
    factor = 1.0 / math.sqrt(tokens * lax.axis_size("shard"))
    b16, f32 = jnp.bfloat16, jnp.float32
    vmem, dma = pltpu.VMEM, pltpu.SemaphoreType.DMA
    n = CHUNKS
    tasks = n + ZFIRST * (ROWS_Y - 1)
    shapes = (
        jax.ShapeDtypeStruct((units, width), b16),
        jax.ShapeDtypeStruct((units, half), f32),
        jax.ShapeDtypeStruct((units, half), f32),
    )
    results = pl.pallas_call(
        functools.partial(kernel, factor),
        out_shape=shapes,
        in_specs=[pl.BlockSpec(memory_space=pl.ANY)] * 7
        + [pl.BlockSpec(memory_space=pltpu.SMEM)],
        out_specs=[pl.BlockSpec(memory_space=pl.ANY)] * 3,
        scratch_shapes=[
            vmem((n, CORES * tokens, cols), b16),
            vmem((n, tokens, cols), b16),
            vmem((tokens, features), b16),
            vmem((features, CORES * tokens), b16),
            vmem((n, features, cols), b16),
            vmem((n - ZFIRST, rows, cols), b16),
            vmem((ZFIRST, CORES * units, cols), b16),
            vmem((tasks, LAYERS_Z - 1, CORES * units, cols), b16),
            vmem((tasks, LAYERS_Z - 1, CORES * units, cols), b16),
            vmem((n, CORES, units, cols), b16),
            vmem((n, units, cols), b16),
            vmem((n, units, cols), b16),
            vmem((n, units, cols), f32),
            vmem((n, units, cols), f32),
            vmem((n, units, cols), f32),
            vmem((n, units, cols), b16),
            vmem((units, width), b16),
            vmem((units, width), f32),
            vmem((units, width), f32),
            vmem((units, half), f32),
            vmem((units, half), f32),
            vmem((units, half), b16),
            dma((n,)), dma((n,)), dma((n,)), dma((n,)), dma((2,)), dma((2,)),
            dma((n,)), dma((n,)), *[dma((tasks, LAYERS_Z - 1))] * 4,
            dma((n,)), dma((n,)), dma((n,)), dma((n,)),
            dma((n,)), dma((n,)), dma, dma, dma((6,)), dma((3, n)),
        ],
        compiler_params=pltpu.CompilerParams(
            collective_id=0, has_side_effects=True, vmem_limit_bytes=56 * 2**20
        ),
        cost_estimate=pl.CostEstimate(
            flops=2 * tokens * width * features, bytes_accessed=24 * 2**20, transcendentals=0
        ),
    )(
        acts, out_grads, local_weight[0], adam_mean[0], adam_var[0],
        global_weight, outer_momentum, step_count,
    )
    return pl.pallas_call(
        place,
        out_shape=shapes,
        in_specs=[pl.BlockSpec(memory_space=pl.ANY)] * 3,
        out_specs=[pl.BlockSpec(memory_space=pl.ANY)] * 3,
        scratch_shapes=[vmem(x.shape, x.dtype) for x in shapes] + [dma((2, 3)), dma((2, 3))],
        compiler_params=pltpu.CompilerParams(vmem_limit_bytes=56 * 2**20),
    )(*results)


def solution(mesh):
    placed = (
        P(("worker", "shard"), None),
        P(("worker", "shard"), None),
        P("worker", "shard", None),
        P("worker", "shard", None),
        P("worker", "shard", None),
        P("shard", "worker"),
        P("shard", "worker"),
        P(),
    )
    grid = (2, CORES * ROWS_Y * LAYERS_Z)
    return jax.shard_map(
        fused if (mesh.shape["worker"], mesh.shape["shard"]) == grid else plain,
        mesh=mesh,
        in_specs=placed,
        out_specs=(P("shard", None), P("shard", "worker"), P("shard", "worker")),
        check_vma=False,
    )
```

```python
import functools
import math

import jax
import jax.numpy as jnp
from jax import lax
from jax.experimental import pallas as pl
from jax.experimental.pallas import tpu as pltpu
from jax.sharding import PartitionSpec as P

CORES = 2
ROWS_Y = 2
LAYERS_Z = 4
CHUNKS = 16
ZFIRST = 3
AHEAD = 3
LAG_Y = 3
LAG_Z = 6
LAG_DONE = 11


def inner_step(weight, mean, var, grad, count):
    moment = 0.9 * mean + 0.1 * grad
    second = 0.95 * var + 0.05 * grad * grad
    first_fix = 1.0 - jnp.power(0.9, count)
    second_fix = 1.0 - jnp.power(0.95, count)
    ratio = moment / first_fix / (jnp.sqrt(second / second_fix) + 1e-08)
    return weight - 0.1 * (ratio + 0.1 * weight)


def plain(
    acts, out_grads, local_weight, adam_mean, adam_var, global_weight, outer_momentum, step_count
):
    shards = lax.axis_size("shard")
    workers = lax.axis_size("worker")
    factor = 1.0 / math.sqrt(acts.shape[0] * shards)
    count = step_count[0].astype(jnp.float32)
    term = lax.dot_general(
        out_grads, acts, (((0,), (0,)), ((), ())), preferred_element_type=jnp.float32
    )
    grad = lax.psum_scatter(
        (term * factor).astype(jnp.bfloat16), "shard", scatter_dimension=0, tiled=True
    ).astype(jnp.float32)
    weight = local_weight[0].astype(jnp.float32)
    stepped = inner_step(weight, adam_mean[0], adam_var[0], grad, count)
    summed = lax.psum_scatter(stepped, "worker", scatter_dimension=1, tiled=True)
    delta = global_weight - summed / workers
    momentum = 0.9 * outer_momentum + delta
    updated = global_weight - 0.7 * (delta + 0.9 * momentum)
    synced = lax.all_gather(updated.astype(jnp.bfloat16), "worker", axis=1, tiled=True)
    return (synced, updated, momentum)


def kernel(
    factor, acts, grads, weight, mean, var, glob, outer, count,
    synced, new_glob, new_mom,
    a, stage, g, gt, p, yin, ybin, lin, rin_z, gbuf, rout, rin, acc, ng, nm, sy, wv, mv, vv, gv, ov, wo,
    a_loc, st_loc, a_out, a_in, gt_out, gt_in, y_out, y_in, rz_out, rz_in, lz_out, lz_in, c_out, c_in, r_out, r_in,
    s_out, s_in, w_out, w_in, loads, stores,
):
    r = lax.axis_index("worker")
    s = lax.axis_index("shard")
    z = lax.div(s, 4)
    y = lax.rem(lax.div(s, 2), 2)
    k = lax.rem(s, 2)
    tokens = acts.shape[0]
    chunks, _, cols = a.shape
    half = chunks * cols
    rows = yin.shape[1]
    units = gbuf.shape[2]
    block = CORES * units
    other_core = (r, z * 4 + y * 2 + 1 - k)
    other_y = (r, z * 4 + (1 - y) * 2 + k)
    other_worker = (1 - r, s)
    firsts = chunks - yin.shape[0]
    plains = chunks - firsts

    def remote(src, dst, send, recv, to):
        return pltpu.make_async_remote_copy(
            src_ref=src, dst_ref=dst, send_sem=send, recv_sem=recv,
            device_id=to, device_id_type=pl.DeviceIdType.MESH,
        )

    def at(start, step=cols):
        return pl.ds(pl.multiple_of(start, step), step)

    def acts_local(c):
        return pltpu.make_async_copy(
            acts.at[:, at(k * half + c * cols)], a.at[c, pl.ds(0, tokens)], a_loc.at[c]
        )

    def acts_staged(c):
        return pltpu.make_async_copy(
            acts.at[:, at((1 - k) * half + c * cols)], stage.at[c], st_loc.at[c]
        )

    def acts_remote(c):
        return remote(
            stage.at[c], a.at[c, pl.ds(tokens, tokens)], a_out.at[c], a_in.at[c], other_core
        )

    def load_acts(c):
        acts_staged(c).start()
        acts_local(c).start()

    def send_acts(c):
        acts_staged(c).wait()
        acts_remote(c).start()

    def y_copy(c):
        return remote(
            p.at[c, at((1 - y) * rows, rows)], yin.at[c], y_out.at[c], y_in.at[c], other_y
        )

    def late_y_copy(c):
        return remote(
            p.at[c, at((1 - y) * rows + z * block, block)], ybin.at[c - plains],
            y_out.at[c], y_in.at[c], other_y,
        )

    def right_copy(task, c, part, here, t):
        return remote(
            p.at[c, at(part * rows + t * block, block)], rin_z.at[task, t - 1],
            rz_out.at[task, t - 1], rz_in.at[task, t - 1], (r, (here + 1) * 4 + y * 2 + k),
        )

    def left_copy(task, c, part, here, t):
        return remote(
            p.at[c, at(part * rows + t * block, block)], lin.at[task, t],
            lz_out.at[task, t], lz_in.at[task, t], (r, (here - 1) * 4 + y * 2 + k),
        )

    def add_to(c, part, low, high, *arrived):
        where = pl.ds(pl.multiple_of(part * rows + low * block, block), (high - low) * block)
        value = p[c, where].astype(jnp.float32)
        for ref in arrived:
            value += ref.astype(jnp.float32)
        p[c, where] = value.astype(jnp.bfloat16)

    def pass_right(task, c, part, here, t):
        right_copy(task, c, part, here - 1, t).wait_recv()
        add_to(c, part, t, t + 1, rin_z[task, t - 1])
        right_copy(task, c, part, here, t).start()

    def pass_left(task, c, part, here, t):
        left_copy(task, c, part, here + 1, t).wait_recv()
        add_to(c, part, t, t + 1, lin[task, t])
        left_copy(task, c, part, here, t).start()

    def line_start(task, c, part):
        @pl.when(z == 0)
        def _():
            for t in (3, 2, 1):
                right_copy(task, c, part, 0, t).start()

        @pl.when(z == 3)
        def _():
            for t in (0, 1, 2):
                left_copy(task, c, part, 3, t).start()

    def line_inward(task, c, part):
        @pl.when(z == 1)
        def _():
            for t in (3, 2):
                pass_right(task, c, part, 1, t)

        @pl.when(z == 2)
        def _():
            for t in (0, 1):
                pass_left(task, c, part, 2, t)

    def line_outward(task, c, part):
        @pl.when(z == 1)
        def _():
            pass_left(task, c, part, 1, 0)

        @pl.when(z == 2)
        def _():
            pass_right(task, c, part, 2, 3)

    def line_end(task, c, part):
        for here in range(LAYERS_Z):

            @pl.when(z == here)
            def _(here=here):
                arrived = []
                if here > 0:
                    right_copy(task, c, part, here - 1, here).wait_recv()
                    arrived.append(rin_z[task, here - 1])
                if here < LAYERS_Z - 1:
                    left_copy(task, c, part, here + 1, here).wait_recv()
                    arrived.append(lin[task, here])
                add_to(c, part, here, here + 1, *arrived)

    def line_sent(task, c, part):
        for here in range(LAYERS_Z):

            @pl.when(z == here)
            def _(here=here):
                for t in range(LAYERS_Z):
                    if t > here:
                        right_copy(task, c, part, here, t).wait_send()
                    if t < here:
                        left_copy(task, c, part, here, t).wait_send()

    def core_copy(c):
        return remote(
            p.at[c, at(y * rows + z * block + (1 - k) * units, units)], gbuf.at[c, k],
            c_out.at[c], c_in.at[c], other_core,
        )

    def ratio_copy(c):
        return remote(rout.at[c], rin.at[c], r_out.at[c], r_in.at[c], other_worker)

    def synced_copy(c):
        return remote(
            sy.at[c], synced.at[:, at(r * half + c * cols)], s_out.at[c], s_in.at[c], other_worker
        )

    def stores_of(c):
        return [
            pltpu.make_async_copy(sy.at[c], synced.at[:, at(r * half + c * cols)], stores.at[0, c]),
            pltpu.make_async_copy(ng.at[c], new_glob.at[:, at(c * cols)], stores.at[1, c]),
            pltpu.make_async_copy(nm.at[c], new_mom.at[:, at(c * cols)], stores.at[2, c]),
        ]

    grads_in = pltpu.make_async_copy(grads, g, loads.at[0])
    grads_in.start()

    load_acts(0)
    load_acts(1)
    load_acts(plains)

    others = [
        pltpu.make_async_copy(x, v, loads.at[1 + j])
        for j, (x, v) in enumerate(
            ((weight, wv), (mean, mv), (var, vv), (glob, gv), (outer, ov))
        )
    ]
    barrier = pltpu.get_barrier_semaphore()
    for peer in (other_core, other_y, other_worker):
        pl.semaphore_signal(barrier, inc=1, device_id=peer, device_id_type=pl.DeviceIdType.MESH)

    @pl.when(z > 0)
    def _():
        pl.semaphore_signal(
            barrier, inc=1, device_id=(r, s - 4), device_id_type=pl.DeviceIdType.MESH
        )

    @pl.when(z < 3)
    def _():
        pl.semaphore_signal(
            barrier, inc=1, device_id=(r, s + 4), device_id_type=pl.DeviceIdType.MESH
        )

    grads_in.wait()
    for j in range(g.shape[1] // block):
        place = (j % ROWS_Y) * LAYERS_Z + j // ROWS_Y
        gt[place * block : (place + 1) * block, 0:tokens] = g[:, j * block : (j + 1) * block].T
    def gt_copy(side):
        where = at(side * rows, rows)
        return remote(
            gt.at[where, pl.ds(0, tokens)], gt.at[where, pl.ds(tokens, tokens)],
            gt_out.at[side], gt_in.at[side], other_core,
        )

    weight_copy = remote(
        wv.at[:, at((1 - r) * half, half)], wo, w_out, w_in, other_worker
    )
    pl.semaphore_wait(barrier, 4 + lax.rem(lax.div(z + 1, 2), 2))
    gt_copy(1 - y).start()

    send_acts(0)
    gt_copy(y).start()
    send_acts(plains)
    send_acts(1)

    @pl.loop(2, plains)
    def _(c):
        load_acts(c)

    @pl.loop(plains + 1, chunks)
    def _(c):
        load_acts(c)

    send_acts(2)
    gt_copy(1 - y).wait_recv()

    time = jnp.full((1, cols), count[0].astype(jnp.float32))
    first = 1.0 / (1.0 - jnp.exp(time * math.log(0.9)))
    second_inv = 1.0 / (1.0 - jnp.exp(time * math.log(0.95)))

    def ratio_of(c, side):
        where = at(side * half + c * cols)
        grad = gbuf[c, side].astype(jnp.float32) * factor
        moment = 0.9 * mv[:, where] + 0.1 * grad
        second = 0.95 * vv[:, where] + 0.05 * grad * grad
        return moment * first / (jnp.sqrt(second * second_inv) + 1e-08)

    def product(c, side):
        p[c, at(side * rows, rows)] = jnp.dot(
            gt[at(side * rows, rows)], a[c], preferred_element_type=jnp.float32
        ).astype(jnp.bfloat16)

    def fetched(c):
        acts_local(c).wait()
        acts_remote(c).wait_recv()

    def to_core(c):
        core_copy(c).start()
        gbuf[c, k] = p[c, at(y * rows + z * block + k * units, units)]

    def adam(c):
        core_copy(c).wait_recv()
        rout[c] = ratio_of(c, 1 - r).astype(jnp.bfloat16)
        ratio_copy(c).start()
        own = wv[:, at(r * half + c * cols)].astype(jnp.float32)
        acc[c] = own - 0.1 * (ratio_of(c, r) + 0.1 * own)

    def update(c):
        ratio_copy(c).wait_recv()
        where = at(c * cols)
        its = wo[:, where].astype(jnp.float32)
        summed = acc[c] + (its - 0.1 * (rin[c].astype(jnp.float32) + 0.1 * its))
        delta = gv[:, where] - summed * 0.5
        momentum = 0.9 * ov[:, where] + delta
        updated = gv[:, where] - 0.7 * (delta + 0.9 * momentum)
        sy[c] = updated.astype(jnp.bfloat16)
        synced_copy(c).start()
        ng[c] = updated
        nm[c] = momentum
        for copy in stores_of(c):
            copy.start()

    def done(c):
        acts_remote(c).wait_send()
        core_copy(c).wait_send()
        ratio_copy(c).wait_send()
        synced_copy(c).wait()
        for copy in stores_of(c):
            copy.wait()

    @pl.loop(0, plains + LAG_DONE)
    def _(i):
        def plain_at(lag):
            def run(stage):
                pl.when((i >= lag) & (i < plains + lag))(lambda: stage(i - lag))
            return run

        def first_at(lag):
            def run(stage):
                pl.when((i >= lag) & (i < firsts + lag))(lambda: stage(i - lag + plains))
            return run

        def halves(stage, c):
            for h in range(ROWS_Y):
                task = plains + (c - plains) * ROWS_Y + h
                stage(task, c, y if h == 1 else 1 - y)

        @plain_at(0)
        def _(c):
            fetched(c)
            product(c, 1 - y)
            y_copy(c).start()

        @pl.when(i == 0)
        def _():
            gt_copy(y).wait_recv()

        @first_at(0)
        def _(c):
            fetched(c)
            for h, part in enumerate((1 - y, y)):
                product(c, part)
                line_start(plains + (c - plains) * ROWS_Y + h, c, part)

        @plain_at(0)
        def _(c):
            product(c, y)

        @pl.when(i + AHEAD < plains)
        def _():
            send_acts(i + AHEAD)

        @pl.when(i < firsts - 1)
        def _():
            send_acts(plains + 1 + i)

        @pl.when(i == 1)
        def _():
            for copy in others:
                copy.start()

        @pl.when(i == 3)
        def _():
            for copy in others:
                copy.wait()
            weight_copy.start()

        @first_at(plains)
        def _(c):
            late_y_copy(c).start()

        @plain_at(LAG_Y)
        def _(c):
            y_copy(c).wait_recv()
            add_to(c, y, 0, LAYERS_Z, yin[c])
            line_start(c, c, y)

        @first_at(plains + LAG_Y + 1)
        def _(c):
            late_y_copy(c).wait_recv()
            where = at(y * rows + z * block, block)
            p[c, where] = (
                p[c, where].astype(jnp.float32) + ybin[c - plains].astype(jnp.float32)
            ).astype(jnp.bfloat16)
            to_core(c)

        @first_at(plains + LAG_Y + 2)
        def _(c):
            adam(c)

        @first_at(plains + LAG_Y + 3)
        def _(c):
            update(c)

        @first_at(plains + LAG_Y + 4)
        def _(c):
            late_y_copy(c).wait_send()
            halves(line_sent, c)
            done(c)

        @first_at(4)
        def _(c):
            halves(line_inward, c)

        @plain_at(LAG_Z)
        def _(c):
            line_inward(c, c, y)

        @first_at(6)
        def _(c):
            halves(line_outward, c)

        @plain_at(LAG_Z + 1)
        def _(c):
            line_outward(c, c, y)

        @first_at(8)
        def _(c):
            halves(line_end, c)

        @plain_at(LAG_Z + 2)
        def _(c):
            line_end(c, c, y)
            to_core(c)

        @pl.when(i == LAG_Z + 3)
        def _():
            weight_copy.wait()

        @plain_at(LAG_Z + 3)
        def _(c):
            adam(c)

        @plain_at(LAG_Z + 4)
        def _(c):
            update(c)

        @plain_at(LAG_DONE)
        def _(c):
            y_copy(c).wait_send()
            line_sent(c, c, y)
            done(c)

    gt_copy(0).wait_send()
    gt_copy(1).wait_send()


def place(a, b, c, to_a, to_b, to_c, held_a, held_b, held_c, sems, out_sems):
    pieces = 2
    loads, stores = [], []
    for p in range(pieces):
        for j, (x, held, to) in enumerate(
            ((a, held_a, to_a), (b, held_b, to_b), (c, held_c, to_c))
        ):
            size = x.shape[0] // pieces
            rows = pl.ds(p * size, size)
            loads.append(pltpu.make_async_copy(x.at[rows], held.at[rows], sems.at[p, j]))
            stores.append(pltpu.make_async_copy(held.at[rows], to.at[rows], out_sems.at[p, j]))
    for copy in loads:
        copy.start()
    for load, store in zip(loads, stores):
        load.wait()
        store.start()
    for copy in stores:
        copy.wait()


def fused(
    acts, out_grads, local_weight, adam_mean, adam_var, global_weight, outer_momentum, step_count
):
    tokens, width = acts.shape
    features = out_grads.shape[1]
    units = local_weight.shape[1]
    half = width // CORES
    cols = half // CHUNKS
    rows = features // ROWS_Y
    factor = 1.0 / math.sqrt(tokens * lax.axis_size("shard"))
    b16, f32 = jnp.bfloat16, jnp.float32
    vmem, dma = pltpu.VMEM, pltpu.SemaphoreType.DMA
    n = CHUNKS
    tasks = n + ZFIRST * (ROWS_Y - 1)
    shapes = (
        jax.ShapeDtypeStruct((units, width), b16),
        jax.ShapeDtypeStruct((units, half), f32),
        jax.ShapeDtypeStruct((units, half), f32),
    )
    results = pl.pallas_call(
        functools.partial(kernel, factor),
        out_shape=shapes,
        in_specs=[pl.BlockSpec(memory_space=pl.ANY)] * 7
        + [pl.BlockSpec(memory_space=pltpu.SMEM)],
        out_specs=[pl.BlockSpec(memory_space=pl.ANY)] * 3,
        scratch_shapes=[
            vmem((n, CORES * tokens, cols), b16),
            vmem((n, tokens, cols), b16),
            vmem((tokens, features), b16),
            vmem((features, CORES * tokens), b16),
            vmem((n, features, cols), b16),
            vmem((n - ZFIRST, rows, cols), b16),
            vmem((ZFIRST, CORES * units, cols), b16),
            vmem((tasks, LAYERS_Z - 1, CORES * units, cols), b16),
            vmem((tasks, LAYERS_Z - 1, CORES * units, cols), b16),
            vmem((n, CORES, units, cols), b16),
            vmem((n, units, cols), b16),
            vmem((n, units, cols), b16),
            vmem((n, units, cols), f32),
            vmem((n, units, cols), f32),
            vmem((n, units, cols), f32),
            vmem((n, units, cols), b16),
            vmem((units, width), b16),
            vmem((units, width), f32),
            vmem((units, width), f32),
            vmem((units, half), f32),
            vmem((units, half), f32),
            vmem((units, half), b16),
            dma((n,)), dma((n,)), dma((n,)), dma((n,)), dma((2,)), dma((2,)),
            dma((n,)), dma((n,)), *[dma((tasks, LAYERS_Z - 1))] * 4,
            dma((n,)), dma((n,)), dma((n,)), dma((n,)),
            dma((n,)), dma((n,)), dma, dma, dma((6,)), dma((3, n)),
        ],
        compiler_params=pltpu.CompilerParams(
            collective_id=0, has_side_effects=True, vmem_limit_bytes=56 * 2**20
        ),
        cost_estimate=pl.CostEstimate(
            flops=2 * tokens * width * features, bytes_accessed=24 * 2**20, transcendentals=0
        ),
    )(
        acts, out_grads, local_weight[0], adam_mean[0], adam_var[0],
        global_weight, outer_momentum, step_count,
    )
    return pl.pallas_call(
        place,
        out_shape=shapes,
        in_specs=[pl.BlockSpec(memory_space=pl.ANY)] * 3,
        out_specs=[pl.BlockSpec(memory_space=pl.ANY)] * 3,
        scratch_shapes=[vmem(x.shape, x.dtype) for x in shapes] + [dma((2, 3)), dma((2, 3))],
        compiler_params=pltpu.CompilerParams(vmem_limit_bytes=56 * 2**20),
    )(*results)


def solution(mesh):
    placed = (
        P(("worker", "shard"), None),
        P(("worker", "shard"), None),
        P("worker", "shard", None),
        P("worker", "shard", None),
        P("worker", "shard", None),
        P("shard", "worker"),
        P("shard", "worker"),
        P(),
    )
    grid = (2, CORES * ROWS_Y * LAYERS_Z)
    return jax.shard_map(
        fused if (mesh.shape["worker"], mesh.shape["shard"]) == grid else plain,
        mesh=mesh,
        in_specs=placed,
        out_specs=(P("shard", None), P("shard", "worker"), P("shard", "worker")),
        check_vma=False,
    )
```

```python
import functools
import math

import jax
import jax.numpy as jnp
from jax import lax
from jax.experimental import pallas as pl
from jax.experimental.pallas import tpu as pltpu
from jax.sharding import PartitionSpec as P

CORES = 2
ROWS_Y = 2
LAYERS_Z = 4
CHUNKS = 16
ZFIRST = 2
AHEAD = 3
LAG_Y = 3
LAG_Z = 6
LAG_DONE = 11


def inner_step(weight, mean, var, grad, count):
    moment = 0.9 * mean + 0.1 * grad
    second = 0.95 * var + 0.05 * grad * grad
    first_fix = 1.0 - jnp.power(0.9, count)
    second_fix = 1.0 - jnp.power(0.95, count)
    ratio = moment / first_fix / (jnp.sqrt(second / second_fix) + 1e-08)
    return weight - 0.1 * (ratio + 0.1 * weight)


def plain(
    acts, out_grads, local_weight, adam_mean, adam_var, global_weight, outer_momentum, step_count
):
    shards = lax.axis_size("shard")
    workers = lax.axis_size("worker")
    factor = 1.0 / math.sqrt(acts.shape[0] * shards)
    count = step_count[0].astype(jnp.float32)
    term = lax.dot_general(
        out_grads, acts, (((0,), (0,)), ((), ())), preferred_element_type=jnp.float32
    )
    grad = lax.psum_scatter(
        (term * factor).astype(jnp.bfloat16), "shard", scatter_dimension=0, tiled=True
    ).astype(jnp.float32)
    weight = local_weight[0].astype(jnp.float32)
    stepped = inner_step(weight, adam_mean[0], adam_var[0], grad, count)
    summed = lax.psum_scatter(stepped, "worker", scatter_dimension=1, tiled=True)
    delta = global_weight - summed / workers
    momentum = 0.9 * outer_momentum + delta
    updated = global_weight - 0.7 * (delta + 0.9 * momentum)
    synced = lax.all_gather(updated.astype(jnp.bfloat16), "worker", axis=1, tiled=True)
    return (synced, updated, momentum)


def kernel(
    factor, acts, grads, weight, mean, var, glob, outer, count,
    synced, new_glob, new_mom,
    a, stage, g, gt, p, yin, ybin, lin, rin_z, gbuf, rout, rin, acc, ng, nm, sy, wv, mv, vv, gv, ov, wo,
    a_loc, st_loc, a_out, a_in, gt_out, gt_in, y_out, y_in, rz_out, rz_in, lz_out, lz_in, c_out, c_in, r_out, r_in,
    s_out, s_in, w_out, w_in, loads, stores,
):
    r = lax.axis_index("worker")
    s = lax.axis_index("shard")
    z = lax.div(s, 4)
    y = lax.rem(lax.div(s, 2), 2)
    k = lax.rem(s, 2)
    tokens = acts.shape[0]
    chunks, _, cols = a.shape
    half = chunks * cols
    rows = yin.shape[1]
    units = gbuf.shape[2]
    block = CORES * units
    other_core = (r, z * 4 + y * 2 + 1 - k)
    other_y = (r, z * 4 + (1 - y) * 2 + k)
    other_worker = (1 - r, s)
    firsts = chunks - yin.shape[0]
    plains = chunks - firsts

    def remote(src, dst, send, recv, to):
        return pltpu.make_async_remote_copy(
            src_ref=src, dst_ref=dst, send_sem=send, recv_sem=recv,
            device_id=to, device_id_type=pl.DeviceIdType.MESH,
        )

    def at(start, step=cols):
        return pl.ds(pl.multiple_of(start, step), step)

    def acts_local(c):
        return pltpu.make_async_copy(
            acts.at[:, at(k * half + c * cols)], a.at[c, pl.ds(0, tokens)], a_loc.at[c]
        )

    def acts_staged(c):
        return pltpu.make_async_copy(
            acts.at[:, at((1 - k) * half + c * cols)], stage.at[c], st_loc.at[c]
        )

    def acts_remote(c):
        return remote(
            stage.at[c], a.at[c, pl.ds(tokens, tokens)], a_out.at[c], a_in.at[c], other_core
        )

    def load_acts(c):
        acts_staged(c).start()
        acts_local(c).start()

    def send_acts(c):
        acts_staged(c).wait()
        acts_remote(c).start()

    def y_copy(c):
        return remote(
            p.at[c, at((1 - y) * rows, rows)], yin.at[c], y_out.at[c], y_in.at[c], other_y
        )

    def late_y_copy(c):
        return remote(
            p.at[c, at((1 - y) * rows + z * block, block)], ybin.at[c - plains],
            y_out.at[c], y_in.at[c], other_y,
        )

    def right_copy(task, c, part, here, t):
        return remote(
            p.at[c, at(part * rows + t * block, block)], rin_z.at[task, t - 1],
            rz_out.at[task, t - 1], rz_in.at[task, t - 1], (r, (here + 1) * 4 + y * 2 + k),
        )

    def left_copy(task, c, part, here, t):
        return remote(
            p.at[c, at(part * rows + t * block, block)], lin.at[task, t],
            lz_out.at[task, t], lz_in.at[task, t], (r, (here - 1) * 4 + y * 2 + k),
        )

    def add_to(c, part, low, high, *arrived):
        where = pl.ds(pl.multiple_of(part * rows + low * block, block), (high - low) * block)
        value = p[c, where].astype(jnp.float32)
        for ref in arrived:
            value += ref.astype(jnp.float32)
        p[c, where] = value.astype(jnp.bfloat16)

    def pass_right(task, c, part, here, t):
        right_copy(task, c, part, here - 1, t).wait_recv()
        add_to(c, part, t, t + 1, rin_z[task, t - 1])
        right_copy(task, c, part, here, t).start()

    def pass_left(task, c, part, here, t):
        left_copy(task, c, part, here + 1, t).wait_recv()
        add_to(c, part, t, t + 1, lin[task, t])
        left_copy(task, c, part, here, t).start()

    def line_start(task, c, part):
        @pl.when(z == 0)
        def _():
            for t in (3, 2, 1):
                right_copy(task, c, part, 0, t).start()

        @pl.when(z == 3)
        def _():
            for t in (0, 1, 2):
                left_copy(task, c, part, 3, t).start()

    def line_inward(task, c, part):
        @pl.when(z == 1)
        def _():
            for t in (3, 2):
                pass_right(task, c, part, 1, t)

        @pl.when(z == 2)
        def _():
            for t in (0, 1):
                pass_left(task, c, part, 2, t)

    def line_outward(task, c, part):
        @pl.when(z == 1)
        def _():
            pass_left(task, c, part, 1, 0)

        @pl.when(z == 2)
        def _():
            pass_right(task, c, part, 2, 3)

    def line_end(task, c, part):
        for here in range(LAYERS_Z):

            @pl.when(z == here)
            def _(here=here):
                arrived = []
                if here > 0:
                    right_copy(task, c, part, here - 1, here).wait_recv()
                    arrived.append(rin_z[task, here - 1])
                if here < LAYERS_Z - 1:
                    left_copy(task, c, part, here + 1, here).wait_recv()
                    arrived.append(lin[task, here])
                add_to(c, part, here, here + 1, *arrived)

    def line_sent(task, c, part):
        for here in range(LAYERS_Z):

            @pl.when(z == here)
            def _(here=here):
                for t in range(LAYERS_Z):
                    if t > here:
                        right_copy(task, c, part, here, t).wait_send()
                    if t < here:
                        left_copy(task, c, part, here, t).wait_send()

    def core_copy(c):
        return remote(
            p.at[c, at(y * rows + z * block + (1 - k) * units, units)], gbuf.at[c, k],
            c_out.at[c], c_in.at[c], other_core,
        )

    def ratio_copy(c):
        return remote(rout.at[c], rin.at[c], r_out.at[c], r_in.at[c], other_worker)

    def synced_copy(c):
        return remote(
            sy.at[c], synced.at[:, at(r * half + c * cols)], s_out.at[c], s_in.at[c], other_worker
        )

    def stores_of(c):
        return [
            pltpu.make_async_copy(sy.at[c], synced.at[:, at(r * half + c * cols)], stores.at[0, c]),
            pltpu.make_async_copy(ng.at[c], new_glob.at[:, at(c * cols)], stores.at[1, c]),
            pltpu.make_async_copy(nm.at[c], new_mom.at[:, at(c * cols)], stores.at[2, c]),
        ]

    grads_in = pltpu.make_async_copy(grads, g, loads.at[0])
    grads_in.start()

    load_acts(0)
    load_acts(1)
    load_acts(plains)

    others = [
        pltpu.make_async_copy(x, v, loads.at[1 + j])
        for j, (x, v) in enumerate(
            ((weight, wv), (mean, mv), (var, vv), (glob, gv), (outer, ov))
        )
    ]
    barrier = pltpu.get_barrier_semaphore()
    for peer in (other_core, other_y, other_worker):
        pl.semaphore_signal(barrier, inc=1, device_id=peer, device_id_type=pl.DeviceIdType.MESH)

    @pl.when(z > 0)
    def _():
        pl.semaphore_signal(
            barrier, inc=1, device_id=(r, s - 4), device_id_type=pl.DeviceIdType.MESH
        )

    @pl.when(z < 3)
    def _():
        pl.semaphore_signal(
            barrier, inc=1, device_id=(r, s + 4), device_id_type=pl.DeviceIdType.MESH
        )

    grads_in.wait()
    for j in range(g.shape[1] // block):
        place = (j % ROWS_Y) * LAYERS_Z + j // ROWS_Y
        gt[place * block : (place + 1) * block, 0:tokens] = g[:, j * block : (j + 1) * block].T
    def gt_copy(side):
        where = at(side * rows, rows)
        return remote(
            gt.at[where, pl.ds(0, tokens)], gt.at[where, pl.ds(tokens, tokens)],
            gt_out.at[side], gt_in.at[side], other_core,
        )

    weight_copy = remote(
        wv.at[:, at((1 - r) * half, half)], wo, w_out, w_in, other_worker
    )
    pl.semaphore_wait(barrier, 4 + lax.rem(lax.div(z + 1, 2), 2))
    gt_copy(1 - y).start()

    send_acts(0)
    gt_copy(y).start()
    send_acts(plains)
    send_acts(1)

    @pl.loop(2, plains)
    def _(c):
        load_acts(c)

    @pl.loop(plains + 1, chunks)
    def _(c):
        load_acts(c)

    send_acts(2)
    gt_copy(1 - y).wait_recv()

    time = jnp.full((1, cols), count[0].astype(jnp.float32))
    first = 1.0 / (1.0 - jnp.exp(time * math.log(0.9)))
    second_inv = 1.0 / (1.0 - jnp.exp(time * math.log(0.95)))

    def ratio_of(c, side):
        where = at(side * half + c * cols)
        grad = gbuf[c, side].astype(jnp.float32) * factor
        moment = 0.9 * mv[:, where] + 0.1 * grad
        second = 0.95 * vv[:, where] + 0.05 * grad * grad
        return moment * first / (jnp.sqrt(second * second_inv) + 1e-08)

    def product(c, side):
        p[c, at(side * rows, rows)] = jnp.dot(
            gt[at(side * rows, rows)], a[c], preferred_element_type=jnp.float32
        ).astype(jnp.bfloat16)

    def fetched(c):
        acts_local(c).wait()
        acts_remote(c).wait_recv()

    def to_core(c):
        core_copy(c).start()
        gbuf[c, k] = p[c, at(y * rows + z * block + k * units, units)]

    def adam(c):
        core_copy(c).wait_recv()
        rout[c] = ratio_of(c, 1 - r).astype(jnp.bfloat16)
        ratio_copy(c).start()
        own = wv[:, at(r * half + c * cols)].astype(jnp.float32)
        acc[c] = own - 0.1 * (ratio_of(c, r) + 0.1 * own)

    def update(c):
        ratio_copy(c).wait_recv()
        where = at(c * cols)
        its = wo[:, where].astype(jnp.float32)
        summed = acc[c] + (its - 0.1 * (rin[c].astype(jnp.float32) + 0.1 * its))
        delta = gv[:, where] - summed * 0.5
        momentum = 0.9 * ov[:, where] + delta
        updated = gv[:, where] - 0.7 * (delta + 0.9 * momentum)
        sy[c] = updated.astype(jnp.bfloat16)
        synced_copy(c).start()
        ng[c] = updated
        nm[c] = momentum
        for copy in stores_of(c):
            copy.start()

    def done(c):
        acts_remote(c).wait_send()
        core_copy(c).wait_send()
        ratio_copy(c).wait_send()
        synced_copy(c).wait()
        for copy in stores_of(c):
            copy.wait()

    @pl.loop(0, plains + LAG_DONE)
    def _(i):
        def plain_at(lag):
            def run(stage):
                pl.when((i >= lag) & (i < plains + lag))(lambda: stage(i - lag))
            return run

        def first_at(lag):
            def run(stage):
                pl.when((i >= lag) & (i < firsts + lag))(lambda: stage(i - lag + plains))
            return run

        def halves(stage, c):
            for h in range(ROWS_Y):
                task = plains + (c - plains) * ROWS_Y + h
                stage(task, c, y if h == 1 else 1 - y)

        @plain_at(0)
        def _(c):
            fetched(c)
            product(c, 1 - y)
            y_copy(c).start()

        @pl.when(i == 0)
        def _():
            gt_copy(y).wait_recv()

        @first_at(0)
        def _(c):
            fetched(c)
            for h, part in enumerate((1 - y, y)):
                product(c, part)
                line_start(plains + (c - plains) * ROWS_Y + h, c, part)

        @plain_at(0)
        def _(c):
            product(c, y)

        @pl.when(i + AHEAD < plains)
        def _():
            send_acts(i + AHEAD)

        @pl.when(i < firsts - 1)
        def _():
            send_acts(plains + 1 + i)

        @pl.when(i == 1)
        def _():
            for copy in others:
                copy.start()

        @pl.when(i == 3)
        def _():
            for copy in others:
                copy.wait()
            weight_copy.start()

        @first_at(plains)
        def _(c):
            late_y_copy(c).start()

        @plain_at(LAG_Y)
        def _(c):
            y_copy(c).wait_recv()
            add_to(c, y, 0, LAYERS_Z, yin[c])
            line_start(c, c, y)

        @first_at(plains + LAG_Y + 1)
        def _(c):
            late_y_copy(c).wait_recv()
            where = at(y * rows + z * block, block)
            p[c, where] = (
                p[c, where].astype(jnp.float32) + ybin[c - plains].astype(jnp.float32)
            ).astype(jnp.bfloat16)
            to_core(c)

        @first_at(plains + LAG_Y + 2)
        def _(c):
            adam(c)

        @first_at(plains + LAG_Y + 3)
        def _(c):
            update(c)

        @first_at(plains + LAG_Y + 4)
        def _(c):
            late_y_copy(c).wait_send()
            halves(line_sent, c)
            done(c)

        @first_at(4)
        def _(c):
            halves(line_inward, c)

        @plain_at(LAG_Z)
        def _(c):
            line_inward(c, c, y)

        @first_at(6)
        def _(c):
            halves(line_outward, c)

        @plain_at(LAG_Z + 1)
        def _(c):
            line_outward(c, c, y)

        @first_at(8)
        def _(c):
            halves(line_end, c)

        @plain_at(LAG_Z + 2)
        def _(c):
            line_end(c, c, y)
            to_core(c)

        @pl.when(i == LAG_Z + 3)
        def _():
            weight_copy.wait()

        @plain_at(LAG_Z + 3)
        def _(c):
            adam(c)

        @plain_at(LAG_Z + 4)
        def _(c):
            update(c)

        @plain_at(LAG_DONE)
        def _(c):
            y_copy(c).wait_send()
            line_sent(c, c, y)
            done(c)

    gt_copy(0).wait_send()
    gt_copy(1).wait_send()


def place(a, b, c, to_a, to_b, to_c, held_a, held_b, held_c, sems, out_sems):
    pieces = 2
    loads, stores = [], []
    for p in range(pieces):
        for j, (x, held, to) in enumerate(
            ((a, held_a, to_a), (b, held_b, to_b), (c, held_c, to_c))
        ):
            size = x.shape[0] // pieces
            rows = pl.ds(p * size, size)
            loads.append(pltpu.make_async_copy(x.at[rows], held.at[rows], sems.at[p, j]))
            stores.append(pltpu.make_async_copy(held.at[rows], to.at[rows], out_sems.at[p, j]))
    for copy in loads:
        copy.start()
    for load, store in zip(loads, stores):
        load.wait()
        store.start()
    for copy in stores:
        copy.wait()


def fused(
    acts, out_grads, local_weight, adam_mean, adam_var, global_weight, outer_momentum, step_count
):
    tokens, width = acts.shape
    features = out_grads.shape[1]
    units = local_weight.shape[1]
    half = width // CORES
    cols = half // CHUNKS
    rows = features // ROWS_Y
    factor = 1.0 / math.sqrt(tokens * lax.axis_size("shard"))
    b16, f32 = jnp.bfloat16, jnp.float32
    vmem, dma = pltpu.VMEM, pltpu.SemaphoreType.DMA
    n = CHUNKS
    tasks = n + ZFIRST * (ROWS_Y - 1)
    shapes = (
        jax.ShapeDtypeStruct((units, width), b16),
        jax.ShapeDtypeStruct((units, half), f32),
        jax.ShapeDtypeStruct((units, half), f32),
    )
    results = pl.pallas_call(
        functools.partial(kernel, factor),
        out_shape=shapes,
        in_specs=[pl.BlockSpec(memory_space=pl.ANY)] * 7
        + [pl.BlockSpec(memory_space=pltpu.SMEM)],
        out_specs=[pl.BlockSpec(memory_space=pl.ANY)] * 3,
        scratch_shapes=[
            vmem((n, CORES * tokens, cols), b16),
            vmem((n, tokens, cols), b16),
            vmem((tokens, features), b16),
            vmem((features, CORES * tokens), b16),
            vmem((n, features, cols), b16),
            vmem((n - ZFIRST, rows, cols), b16),
            vmem((ZFIRST, CORES * units, cols), b16),
            vmem((tasks, LAYERS_Z - 1, CORES * units, cols), b16),
            vmem((tasks, LAYERS_Z - 1, CORES * units, cols), b16),
            vmem((n, CORES, units, cols), b16),
            vmem((n, units, cols), b16),
            vmem((n, units, cols), b16),
            vmem((n, units, cols), f32),
            vmem((n, units, cols), f32),
            vmem((n, units, cols), f32),
            vmem((n, units, cols), b16),
            vmem((units, width), b16),
            vmem((units, width), f32),
            vmem((units, width), f32),
            vmem((units, half), f32),
            vmem((units, half), f32),
            vmem((units, half), b16),
            dma((n,)), dma((n,)), dma((n,)), dma((n,)), dma((2,)), dma((2,)),
            dma((n,)), dma((n,)), *[dma((tasks, LAYERS_Z - 1))] * 4,
            dma((n,)), dma((n,)), dma((n,)), dma((n,)),
            dma((n,)), dma((n,)), dma, dma, dma((6,)), dma((3, n)),
        ],
        compiler_params=pltpu.CompilerParams(
            collective_id=0, has_side_effects=True, vmem_limit_bytes=56 * 2**20
        ),
        cost_estimate=pl.CostEstimate(
            flops=2 * tokens * width * features, bytes_accessed=24 * 2**20, transcendentals=0
        ),
    )(
        acts, out_grads, local_weight[0], adam_mean[0], adam_var[0],
        global_weight, outer_momentum, step_count,
    )
    return pl.pallas_call(
        place,
        out_shape=shapes,
        in_specs=[pl.BlockSpec(memory_space=pl.ANY)] * 3,
        out_specs=[pl.BlockSpec(memory_space=pl.ANY)] * 3,
        scratch_shapes=[vmem(x.shape, x.dtype) for x in shapes] + [dma((2, 3)), dma((2, 3))],
        compiler_params=pltpu.CompilerParams(vmem_limit_bytes=56 * 2**20),
    )(*results)


def solution(mesh):
    placed = (
        P(("worker", "shard"), None),
        P(("worker", "shard"), None),
        P("worker", "shard", None),
        P("worker", "shard", None),
        P("worker", "shard", None),
        P("shard", "worker"),
        P("shard", "worker"),
        P(),
    )
    grid = (2, CORES * ROWS_Y * LAYERS_Z)
    return jax.shard_map(
        fused if (mesh.shape["worker"], mesh.shape["shard"]) == grid else plain,
        mesh=mesh,
        in_specs=placed,
        out_specs=(P("shard", None), P("shard", "worker"), P("shard", "worker")),
        check_vma=False,
    )
```
